256 devices in a mesh: attn: 16 (over x, y_lo, core), ffn: 8 (over z), tp: 2 (over y_hi).
Axes of the slice: x: 4, y: 4 (y_hi: 2, y_lo: 2; y = y_hi * 2 + y_lo), z: 8, core: 2. Of those that a mesh axis runs over, the one named last changes fastest.
Arguments:
- queries: bfloat16 [2, 64, 16384], P(None, 'attn', ('ffn', 'tp')), may hold values from -20 to 20
- new_pairs: bfloat16 [2, 64, 512], P(None, 'attn'), may hold values from -5 to 5
- kv_pool: bfloat16 [1024, 64, 512], P('attn'), may hold values from -5 to 5
- table_first: int32 [64, 16], P('attn'), may hold values from 0 to 47
- table_second: int32 [64, 16], P('attn'), may hold values from 0 to 63
- lengths: int32 [2, 64], P(None, 'attn'), may hold values from 1 to 1024, 32768 in all within a row
- migrations: int32 [16, 16], P('attn'), may hold values from 0 to 47
- residual: bfloat16 [2, 64, 7168], P(None, None, 'attn'), may hold values from -50 to 50
- out_proj: bfloat16 [16384, 7168], P(('ffn', 'tp'), 'attn'), may hold values from -0.75 to 0.75
- norm_gain: bfloat16 [7168], P('attn'), may hold values from 0.25 to 1.75
- router: bfloat16 [7168, 8], P('attn', 'ffn'), may hold values from -0.0625 to 0.0625
- routes: int32 [2, 64, 3], replicated, may hold values from 0 to 7, all different within a row; in each aligned block of 64 rows (0 to 63, 64 to 127, ..., all dimensions but the last counted through in order) at most 48 rows name the same one
- gate_weight: bfloat16 [8, 7168, 5120], P('ffn', 'attn', 'tp'), may hold values from -0.0625 to 0.0625
- up_weight: bfloat16 [8, 7168, 5120], P('ffn', 'attn', 'tp'), may hold values from -0.0625 to 0.0625
- down_weight: bfloat16 [8, 5120, 7168], P('ffn', 'tp', 'attn'), may hold values from -0.078125 to 0.078125
Outputs:
- mixed: bfloat16 [2, 64, 7168], P(None, ('ffn', 'tp'), 'attn')
The draws below stay inside these ranges and needn't reach their ends.
Inputs may be any that keep to these rules, and one draw needn't show every extreme that they name: `table_first`: local pages of the row's own attention device. `table_second`: local pages of the row's own attention device. `lengths`: the largest length is reached in each step. `migrations`: local pages of the sending device. `routes`: each row names 3 different experts; in each step no expert is named by more than 48 rows, a bound that some block reaches.
All inputs are finite; a program needn't handle non-finite values. No bound on the sum of `lengths` on one device may be relied on, other than what follows from the above.
Results may differ from the reference program's by a relative error of at most 0.023.
Values may be sent and summed in bfloat16 or wider, within the bound.
A program may use at most 64 MiB of HBM per device.

```python
import math
import jax
import jax.numpy as jnp
import numpy as np
from jax import lax

D = 7168
HEADS = 64
HD = 256
FF = 5120
TOPK = 3
ROW_DEV = 4
PAGE = 64
MAXP = 16
PAGES = 64
MCAP = 1
ROWS = 64
EXPERTS = 8
CAP = 48
N_ATTN = 16
N_FFN = 8
N_TP = 2


def token_rows(key, shape):
    noise_key = jax.random.fold_in(key, 0)
    value_key = jax.random.fold_in(key, 2)
    keys = jax.random.truncated_normal(noise_key, -4.0, 4.0, shape + (HD,), jnp.float32)
    values = jax.random.truncated_normal(value_key, -4.0, 4.0, shape + (HD,), jnp.float32)
    return jnp.concatenate([keys, values], axis=-1)


def draw_queries(key, part):
    key = jax.random.fold_in(key, 3)
    noise_key = jax.random.fold_in(key, 0)
    noise = jax.random.truncated_normal(noise_key, -4.0, 4.0, (2, ROWS, HEADS, HD), jnp.float32)
    values = noise
    return values.reshape(2, ROWS, HEADS * HD).astype(jnp.bfloat16)


def draw_new_pairs(key, part):
    key = jax.random.fold_in(key, 5)
    return token_rows(key, (2, ROWS)).astype(jnp.bfloat16)


def draw_kv_pool(key, part):
    key = jax.random.fold_in(key, 7)
    return token_rows(key, (N_ATTN * PAGES, PAGE)).astype(jnp.bfloat16)


def draw_residual(key, part):
    key = jax.random.fold_in(key, 9)
    noise_key, row_key, group_key = jax.random.split(key, 3)
    column = jnp.arange(D, dtype=jnp.float32)
    group_count = D // 64
    factors = jnp.exp(jax.random.uniform(group_key, (group_count,), jnp.float32, -0.7, 0.7))
    column_scale = 3.0 ** (column / D - 0.5) * jnp.repeat(factors, 64)
    row_scale = jnp.exp(jax.random.uniform(row_key, (2, ROWS, 1), jnp.float32, -1.15, 1.15))
    noise = jax.random.truncated_normal(noise_key, -4.0, 4.0, (2, ROWS, D), jnp.float32)
    return (noise * row_scale * column_scale).astype(jnp.bfloat16)


def touch_ends(result, key, smallest, top_value):
    dims = result.shape
    index_at = [jax.random.randint(jax.random.fold_in(key, axis), (), 0, dims[axis]) for axis in range(len(dims))]
    result = result.at[tuple(index_at)].set(smallest)
    longest = dims.index(max(dims))
    index_at[longest] = (index_at[longest] + 1) % dims[longest]
    return result.at[tuple(index_at)].set(top_value)


def steps_of(key, shape, shards, smallest, high):
    level, own = 1.0, jax.random.fold_in(key, 6)
    for axis_at, parts in shards:
        steps = jnp.exp(jax.random.uniform(jax.random.fold_in(own, axis_at), (parts,), jnp.float32, smallest / len(shards), high / len(shards)))
        level = level * jnp.repeat(steps, shape[axis_at] // parts).reshape([-1 if axis == axis_at else 1 for axis in range(len(shape))])
    return level


def split_up(number_of, total, limit, slope):
    loads = [(1 << 20) // math.isqrt(rank ** slope) + 1 for rank in range(2, number_of + 1)]
    rest, holding = total - limit - (number_of - 1), [1] * (number_of - 1)
    while rest > 0:
        candidates = [i for i in range(number_of - 1) if holding[i] < limit]
        mass, budget = sum([loads[i] for i in candidates]), rest
        for i in candidates:
            extra = min(limit - holding[i], max(1, budget * loads[i] // mass), rest)
            holding[i] = holding[i] + extra
            rest = rest - extra
    return np.array([limit] + holding)


def ragged_sizes(rng, amount, total, most, lean):
    if amount == 2:
        one = jax.random.randint(rng, (), max(1, total - most), min(most, total - 1) + 1)
        return jnp.stack([one, total - one])
    tallies = jnp.asarray(split_up(amount, total, most, lean), jnp.int32)
    pairs = (amount - 1) // 2
    giver, sink = tallies[1:1 + 2 * pairs:2], tallies[2:2 + 2 * pairs:2]
    margin = jnp.minimum(giver - 1, most - sink)
    shifted = jax.random.randint(jax.random.fold_in(rng, 1), (pairs,), 0, 1 << 20) % (margin + 1)
    tallies = tallies.at[1:1 + 2 * pairs:2].set(giver - shifted).at[2:2 + 2 * pairs:2].set(sink + shifted)
    return tallies[jax.random.permutation(jax.random.fold_in(rng, 2), amount)]


def deal_out(key, own, number, rows, count, top, bound, lean):
    sequence = jax.random.permutation(key, count)
    heavy_load, usual = shares(count, rows * top, bound, lean, True), shares(count, rows * top, bound, lean, False)
    places = jnp.arange(count)

    def named(sizes, rotation):
        used = int((sizes > 0).sum())
        fixed = max(1, used // 4)
        passed = fixed + (places - fixed + rotation * (used - fixed)) % max(1, count - fixed)
        return jnp.zeros((count,), jnp.int32).at[sequence[jnp.where(places < fixed, places, passed)]].set(jnp.asarray(sizes, jnp.int32))

    sizes = jnp.where(number % 4 == 0, named(heavy_load, number // 4), named(usual, number - number // 4 - 1))
    mixed = jax.random.permutation(jax.random.fold_in(own, 3), count)
    giver, taker = mixed[0:count // 2 * 2:2], mixed[1:count // 2 * 2:2]
    room = jnp.minimum(sizes[giver] - 1, bound - sizes[taker]) // 2
    room = jnp.where((giver == sequence[0]) | (taker == sequence[0]) | (sizes[taker] == 0), 0, jnp.maximum(room, 0))
    passed = jax.random.randint(jax.random.fold_in(own, 4), (count // 2,), 0, 1 << 20) % (room + 1)
    sizes = sizes.at[giver].add(-passed).at[taker].add(passed)
    items = jnp.searchsorted(jnp.cumsum(sizes), jnp.arange(rows * top), side="right").astype(jnp.int32)
    grid = items.reshape(top, rows).T
    grid = grid[jax.random.permutation(jax.random.fold_in(own, 1), rows)]
    rotation = jax.random.randint(jax.random.fold_in(own, 2), (rows, 1), 0, top)
    return jnp.take_along_axis(grid, (jnp.arange(top)[None, :] + rotation) % top, axis=1)


def shares(amount, total, bound, lean, full):
    weights = [(1 << 20) // math.isqrt(rank ** lean) + 1 for rank in range(1, amount + 1)]
    largest = bound if full else min(bound, max(-(-total // amount), total * weights[0] // sum(weights)))
    least = 1 if total - largest >= amount - 1 else 0
    holding, spare = [largest] + [least] * (amount - 1), total - largest - least * (amount - 1)
    while spare > 0:
        free = [i for i in range(1, amount) if holding[i] < largest] or [i for i in range(1, amount) if holding[i] < bound]
        pool, budget = sum([weights[i] for i in free]), spare
        for i in free:
            more = min(bound - holding[i], max(1, budget * weights[i] // pool), spare)
            holding[i] = holding[i] + more
            spare = spare - more
    return np.array(holding)


def centred(own_key, dims, scale, bound, cuts=(), kind=jnp.bfloat16):
    array = jax.random.normal(own_key, dims, jnp.float32) * scale
    if len(cuts) > 0:
        array = steps_of(own_key, dims, cuts, -0.22, 0.18) * array
    return jnp.clip(array, min=-bound, max=bound).astype(kind)


def setup_inputs(seed: int = 0) -> dict:
    seeds = jax.random.split(jax.random.key(seed), 16)
    queries = draw_queries(jax.random.fold_in(seeds[15], 71), 0)
    new_pairs = draw_new_pairs(jax.random.fold_in(seeds[15], 71), 0)
    kv_pool = draw_kv_pool(jax.random.fold_in(seeds[15], 71), 0)
    table_first = touch_ends(jax.random.randint(seeds[3], (ROWS, MAXP), 0, PAGES - N_ATTN * MCAP), jax.random.fold_in(seeds[3], 1), 0, (PAGES - N_ATTN * MCAP) - 1).astype(jnp.int32)
    table_second = touch_ends(jax.random.randint(seeds[4], (ROWS, MAXP), 0, PAGES), jax.random.fold_in(seeds[4], 1), 0, PAGES - 1).astype(jnp.int32)
    lengths = jax.vmap(lambda own: ragged_sizes(own, ROWS, ROWS * MAXP * PAGE // 2, MAXP * PAGE, 1))(jax.random.split(seeds[5], 2)).reshape((2, ROWS)).astype(jnp.int32)
    migrations = touch_ends(jax.random.randint(seeds[6], (N_ATTN, N_ATTN * MCAP), 0, PAGES - N_ATTN * MCAP), jax.random.fold_in(seeds[6], 1), 0, (PAGES - N_ATTN * MCAP) - 1).astype(jnp.int32)
    residual = draw_residual(jax.random.fold_in(seeds[15], 71), 0)
    out_proj = centred(seeds[8], (HEADS * HD, D), HEADS ** -0.5, 0.75, ((0, 16), (1, 16)))
    norm_gain = jnp.clip(1.0 + 0.15 * jax.random.normal(seeds[9], (D,), jnp.float32), 0.25, 1.75).astype(jnp.bfloat16)
    router = centred(seeds[10], (D, EXPERTS), D ** -0.5, 0.0625, ((0, 16), (1, 8)))
    routes_keys = jax.random.split(jax.random.fold_in(seeds[11], 1), 2 * ROWS // ROWS)
    routes_turns = jax.random.permutation(jax.random.fold_in(seeds[11], 3), 2 * ROWS // ROWS)
    routes = jax.vmap(lambda own, number: deal_out(jax.random.fold_in(seeds[11], 2), own, number, ROWS, EXPERTS, TOPK, CAP, 2))(routes_keys, routes_turns).reshape((2, ROWS, TOPK))
    gate_weight = centred(seeds[12], (EXPERTS, D, FF), D ** -0.5, 0.0625, ((0, 8), (1, 16), (2, 2)))
    up_weight = centred(seeds[13], (EXPERTS, D, FF), D ** -0.5, 0.0625, ((0, 8), (1, 16), (2, 2)))
    down_weight = centred(seeds[14], (EXPERTS, FF, D), FF ** -0.5, 0.078125, ((0, 8), (1, 2), (2, 16)))
    return {"queries": queries, "new_pairs": new_pairs, "kv_pool": kv_pool, "table_first": table_first, "table_second": table_second, "lengths": lengths, "migrations": migrations, "residual": residual, "out_proj": out_proj, "norm_gain": norm_gain, "router": router, "routes": routes, "gate_weight": gate_weight, "up_weight": up_weight, "down_weight": down_weight}


EPSILON = 1e-06

def attend(queries, gathered, new_pair, lengths):
    row_count = queries.shape[0]
    tokens = gathered.shape[1]
    query = queries.reshape(row_count, HEADS, HD).astype(jnp.float32)
    keys = jnp.concatenate([gathered[:, :, :HD], new_pair[:, None, :HD]], axis=1).astype(jnp.float32)
    values = jnp.concatenate([gathered[:, :, HD:], new_pair[:, None, HD:]], axis=1).astype(jnp.float32)
    scores = jnp.einsum('rhd,rtd->rht', query, keys) * HD ** (-0.5)
    place = jnp.arange(tokens + 1, dtype=jnp.int32)
    live = (place[None, :] < lengths[:, None]) | (place[None, :] == tokens)
    scores = jnp.where(live[:, None, :], scores, -jnp.inf)
    highest = lax.optimization_barrier(jnp.max(scores, axis=2, keepdims=True))
    weights = jnp.exp(scores - highest)
    denominator = lax.optimization_barrier(jnp.sum(weights, axis=2))
    rounded = lax.optimization_barrier(weights.astype(jnp.bfloat16)).astype(jnp.float32)
    mixed = jnp.einsum('rht,rtd->rhd', rounded, values)
    return (mixed / denominator[:, :, None]).astype(jnp.bfloat16).reshape(row_count, HEADS * HD)

def slot_rows(picks, experts, capacity):
    row_count = picks.shape[0]
    labels = jnp.arange(experts, dtype=jnp.int32)
    chosen = jnp.any(picks[:, :, None] == labels[None, None, :], axis=1)
    ranking = jnp.cumsum(chosen.astype(jnp.int32), axis=0) - 1
    target = jnp.where(chosen, ranking, capacity)
    owner = jnp.broadcast_to(labels[None, :], (row_count, experts))
    source = jnp.broadcast_to(jnp.arange(row_count, dtype=jnp.int32)[:, None], (row_count, experts))
    return jnp.full((experts, capacity), -1, jnp.int32).at[owner, target].set(source, mode='drop')

def to_wire(values):
    return lax.optimization_barrier(values.astype(jnp.bfloat16)).astype(jnp.float32)

def reference(queries, new_pairs, kv_pool, table_first, table_second, lengths, migrations, residual, out_proj, norm_gain, router, routes, gate_weight, up_weight, down_weight):
    groups = N_FFN * N_TP
    incoming = N_ATTN * MCAP
    pools = kv_pool.reshape(N_ATTN, PAGES, PAGE, 2 * HD)
    sent = jax.vmap(lambda page_pool, chosen: page_pool[chosen])(pools, migrations)
    arrived = sent.reshape(N_ATTN, N_ATTN, MCAP, PAGE, 2 * HD).transpose(1, 0, 2, 3, 4).reshape(N_ATTN, incoming, PAGE, 2 * HD)
    new_pool = jnp.concatenate([pools[:, :PAGES - incoming], arrived], axis=1)
    block = HEADS * HD // groups
    half = FF // N_TP
    gain = norm_gain.astype(jnp.float32)
    results = []
    for step_index in range(2):
        pool_set = pools if step_index == 0 else new_pool
        page_table = table_first if step_index == 0 else table_second

        def one_device(inputs):
            page_pool, device_table, device_queries, device_pairs, device_lengths = inputs
            gathered = page_pool[device_table].reshape(ROW_DEV, MAXP * PAGE, 2 * HD)
            return attend(device_queries, gathered, device_pairs, device_lengths)
        attended = lax.map(one_device, (pool_set, page_table.reshape(N_ATTN, ROW_DEV, MAXP), queries[step_index].reshape(N_ATTN, ROW_DEV, HEADS * HD), new_pairs[step_index].reshape(N_ATTN, ROW_DEV, 2 * HD), lengths[step_index].reshape(N_ATTN, ROW_DEV))).reshape(ROWS, HEADS * HD)
        partials = [jnp.dot(attended[:, g * block:(g + 1) * block], out_proj[g * block:(g + 1) * block], preferred_element_type=jnp.float32) for g in range(groups)]
        base = residual[step_index].astype(jnp.float32)
        hidden = base
        for g in range(groups):
            hidden = hidden + to_wire(partials[g])
        slot_table = slot_rows(routes[step_index], EXPERTS, CAP)
        total = base
        for expert in range(EXPERTS):
            chosen = slot_table[expert]
            filled = (chosen >= 0)[:, None]
            slot_index = jnp.maximum(chosen, 0)
            rows_in = jnp.where(filled, hidden[slot_index], 0.0)
            inverse = lax.rsqrt(lax.optimization_barrier(jnp.sum(rows_in * rows_in, axis=1)) / D + EPSILON)[:, None]
            scaled = (rows_in * gain).astype(jnp.bfloat16)
            gate = jnp.dot(scaled, gate_weight[expert], preferred_element_type=jnp.float32) * inverse
            up = jnp.dot(scaled, up_weight[expert], preferred_element_type=jnp.float32) * inverse
            logit = jnp.dot(scaled, router[:, expert], preferred_element_type=jnp.float32)
            route_weight = jax.nn.sigmoid(logit * inverse[:, 0])
            activated = (jax.nn.silu(gate) * up).astype(jnp.bfloat16)
            for part_index in range(N_TP):
                g = expert * N_TP + part_index
                expert_half = jnp.dot(activated[:, part_index * half:(part_index + 1) * half], down_weight[expert, part_index * half:(part_index + 1) * half], preferred_element_type=jnp.float32)
                added = jnp.zeros((ROWS, D), jnp.float32).at[slot_index].add(jnp.where(filled, route_weight[:, None] * expert_half, 0.0))
                total = total + to_wire(partials[g] + added)
        results.append(total.astype(jnp.bfloat16))
    return jnp.stack(results)
```

```python
import jax
import jax.numpy as jnp
from jax import lax
from jax.experimental import pallas as pl
from jax.experimental.pallas import tpu as pltpu
from jax.sharding import PartitionSpec as P

F32, BF16 = jnp.float32, jnp.bfloat16
MESH = pl.DeviceIdType.MESH
D = 7168
EPSILON = 1e-6
NA, NG = 16, 16
CHIPS = 8
LOCAL = 48
PAGE, HD = 64, 256
TOKENS = LOCAL * PAGE
CHUNK = 512
CAP = 48
W = 448
NONE = -1e30
SCALE = HD ** -0.5
NT_DIMS = (((1,), (1,)), ((), ()))
QUERY, PARTIAL, HEADS_OUT, PROJ, ROWS_IN, STATS, SIBLING, REDUCE, ACT, FORWARD, BACK = range(11)


def iota(shape, axis):
    return lax.broadcasted_iota(jnp.int32, shape, axis)


def dot(a, b):
    return jnp.dot(a, b, preferred_element_type=F32)


def dot_nt(a, b):
    return lax.dot_general(a, b, NT_DIMS, preferred_element_type=F32)


def fold(block):
    return jnp.concatenate([block[..., :256], block[..., 256:]], axis=-2)


def unfold(block):
    return jnp.concatenate([block[..., :8, :], block[..., 8:, :]], axis=-1)


def silu(v):
    return v / (1.0 + jnp.exp(-v))


def body(
    queries, new_pairs, kv_pool, table_first, table_second, lengths_in, migrations_in, residual,
    out_proj, norm_gain, router, routes, gate_weight, up_weight, down_weight,
    out,
    lengths, migrations, q_v, pair_v, pool, tab1, tab2, resid_v, wo, gain_v, router_v, routes_v, wg, wu, wd,
    load_sem, send, recv,
    tx1, rx1, tx2, rx2, tx3, rx3, tx4, rx4, tx5, rx5, tx6, rx6, txs, rxs, tx7, rx7, tx8, rx8, tx9, rx9,
    score, hidden_v, slots_v, rows_v, pick, spread, edge, own_v,
):
    me = lax.axis_index("attn")
    expert = lax.axis_index("ffn")
    g_me = expert * 2 + lax.axis_index("tp")
    core = lax.rem(me, 2)
    chip = me // 2
    sibling = me + 1 - 2 * core

    pairs = [
        (queries, q_v), (table_second, tab2), (table_first, tab1), (new_pairs, pair_v),
        (lengths_in, lengths), (migrations_in, migrations),
        (kv_pool.at[pl.ds(0, LOCAL)], pool), (routes, routes_v), (router, router_v), (norm_gain, gain_v),
        (residual, resid_v), (out_proj, wo), (gate_weight.at[0], wg), (up_weight.at[0], wu), (down_weight, wd),
    ]
    loads = [pltpu.make_async_copy(src, dst, load_sem.at[i]) for i, (src, dst) in enumerate(pairs)]
    for load in loads:
        load.start()
    (l_q, l_t2, l_t1, l_pair, l_len, l_mig, l_pool, l_routes, l_router, l_gain, l_resid, l_wo, l_wg, l_wu, l_wd) = loads

    def attn_id(i):
        return {"attn": i}

    def group_id(g):
        return {"ffn": g // 2, "tp": lax.rem(g, 2)}

    barrier = pltpu.get_barrier_semaphore()

    def greet(i, _):
        pl.semaphore_signal(barrier, inc=1, device_id=attn_id(lax.rem(me + i, NA)), device_id_type=MESH)
        pl.semaphore_signal(barrier, inc=1, device_id=group_id(lax.rem(g_me + i, NG)), device_id_type=MESH)
        return 0

    lax.fori_loop(1, NA, greet, 0)

    def remote(phase, src, dst, slot_to, slot_from, device):
        return pltpu.make_async_remote_copy(
            src_ref=src, dst_ref=dst, send_sem=send.at[phase, slot_to], recv_sem=recv.at[phase, slot_from],
            device_id=device, device_id_type=MESH,
        )

    l_q.wait()
    l_t2.wait()
    l_len.wait()
    q8 = jnp.concatenate([q_v[0].astype(F32), q_v[1].astype(F32)], axis=0)
    t2 = tab2[...]
    t2x = jnp.concatenate([t2, t2, t2, t2], axis=0)

    def column(rows, values):
        at = iota((rows, 1), 0)
        result = jnp.zeros((rows, 1), jnp.int32)
        for i in range(rows):
            result = jnp.where(at == i, values[i], result)
        return result

    len2 = column(16, [lengths[1, i % 4] for i in range(16)])
    len8 = column(8, [lengths[i // 4, i % 4] for i in range(8)])

    def counts(table, length, first, width):
        lane = iota((table.shape[0], width), 1)
        page, place = first + lane // PAGE, lane % PAGE
        total = jnp.zeros((table.shape[0], width), F32)
        for k in range(16):
            left = length - k * PAGE
            total = total + jnp.where((page == table[:, k:k + 1]) & (place < left), 1.0, 0.0)
        return total

    q2 = jnp.concatenate([q8[4:8, h * HD:(h + 1) * HD] for h in range(4)], axis=0).astype(BF16)
    for s in range(0, NA, 2):
        c = counts(t2x, len2, LOCAL + s, 2 * PAGE)
        tx1[s, :, 0:HD] = q2
        tx1[s, :, HD:384] = c.astype(BF16)
        tx1[s + 1, :, 0:HD] = q2
        tx1[s + 1, :, HD:384] = pltpu.roll(c, PAGE, axis=1).astype(BF16)
    rx1[me] = tx1[me]

    pl.semaphore_wait(barrier, 2 * (NA - 1))

    def spread_attn(phase, src_of, dst, slot):
        def one(i, _):
            peer = lax.rem(me + i, NA)
            remote(phase, src_of(peer), dst.at[slot], peer, slot, attn_id(peer)).start()
            return 0
        lax.fori_loop(1, NA, one, 0)

    def spread_group(phase, src_of, dst):
        def one(i, _):
            peer = lax.rem(g_me + i, NG)
            remote(phase, src_of(peer), dst.at[g_me], peer, g_me, group_id(peer)).start()
            return 0
        lax.fori_loop(1, NG, one, 0)

    def await_all(phase, src_of, dst, mine):
        def one(i, _):
            peer = lax.rem(mine + i, 16)
            remote(phase, src_of(peer), dst.at[peer], peer, peer, attn_id(me)).wait_recv()
            return 0
        lax.fori_loop(1, 16, one, 0)

    spread_attn(QUERY, lambda peer: tx1.at[peer], rx1, me)

    l_routes.wait()
    l_router.wait()
    named = [routes_v[i] == expert for i in range(3)]
    chosen = jnp.where(named[0] | named[1] | named[2], 1.0, 0.0)
    chosen = jnp.concatenate([chosen[0:1], chosen[1:2]], axis=1)
    row, lane = iota((128, 128), 0), iota((128, 128), 1)
    row_step = (row % 8) // 4
    natural = row_step * 64 + (row // 8) * 4 + row % 4
    chosen_at = jnp.sum(jnp.where(lane == natural, chosen, 0.0), axis=1, keepdims=True)
    before = (lane < natural) & (lane // 64 == row_step)
    rank = jnp.sum(jnp.where(before, chosen, 0.0), axis=1, keepdims=True).astype(jnp.int32)
    slot_at = rank + jnp.where(row_step == core, 0, CAP)
    picked = jnp.where((lane == slot_at) & (chosen_at > 0.5), 1.0, 0.0)
    spread[...] = picked.astype(BF16)
    pick[...] = jnp.transpose(picked)
    router_row = jnp.concatenate([router_v[...].astype(F32), jnp.zeros((1, 512 - W), F32)], axis=1)
    edge_row, edge_lane = iota((8, 512), 0), iota((8, 512), 1)
    edge[...] = jnp.where(
        edge_row == 0, router_row, jnp.where((edge_row == 1) & (edge_lane >= W) & (edge_lane < W + 2), 1.0, 0.0)
    ).astype(BF16)

    l_pool.wait()
    l_mig.wait()

    def serve(i, _):
        source = lax.rem(me + i, NA)

        @pl.when(i > 0)
        def _():
            remote(QUERY, tx1.at[source], rx1.at[source], source, source, attn_id(me)).wait_recv()

        page = migrations[0, source]
        count = rx1[source, :, HD:HD + PAGE].astype(F32)
        live = count > 0.5
        s = dot_nt(rx1[source, :, 0:HD], pool[page, :, 0:HD]) * SCALE
        top = jnp.max(jnp.where(live, s, NONE), axis=1, keepdims=True).astype(BF16).astype(F32)
        weight = jnp.where(live, count * jnp.exp(s - top), 0.0)
        total = jnp.sum(weight, axis=1, keepdims=True)
        high = total.astype(BF16).astype(F32)
        o = dot(weight.astype(BF16), pool[page, :, HD:2 * HD])
        at = iota((16, 128), 1)
        stat = jnp.where(at == 0, top, jnp.where(at == 1, high, jnp.where(at == 2, total - high, 0.0)))
        tx2[source, :, 0:HD] = o.astype(BF16)
        tx2[source, :, HD:384] = stat.astype(BF16)

        @pl.when(i > 0)
        def _():
            remote(PARTIAL, tx2.at[source], rx2.at[me], source, me, attn_id(source)).start()

        return 0

    lax.fori_loop(0, NA, serve, 0)
    rx2[me] = tx2[me]

    l_t1.wait()
    l_pair.wait()
    t8 = jnp.concatenate([tab1[...], t2], axis=0)
    q32 = jnp.concatenate([q8[:, h * HD:(h + 1) * HD] for h in range(4)], axis=0)
    q32b = q32.astype(BF16)
    pair8 = jnp.concatenate([pair_v[0].astype(F32), pair_v[1].astype(F32)], axis=0)
    peak = jnp.full((32, 128), NONE, F32)
    all_counts = []
    for c in range(TOKENS // CHUNK):
        pages = CHUNK // PAGE
        count = counts(t8, len8, c * pages, CHUNK)
        count = jnp.concatenate([count] * 4, axis=0)
        s = dot_nt(q32b, pool[c * pages:(c + 1) * pages, :, 0:HD].reshape(CHUNK, HD)) * SCALE
        s = jnp.where(count > 0.5, s, NONE)
        score[0, :, c * CHUNK:(c + 1) * CHUNK] = s
        score[1, :, c * CHUNK:(c + 1) * CHUNK] = count
        for b in range(CHUNK // 128):
            peak = jnp.maximum(peak, s[:, b * 128:(b + 1) * 128])
    m_local = jnp.max(peak, axis=1, keepdims=True)
    sums = jnp.zeros((32, 128), F32)
    o_local = jnp.zeros((32, HD), F32)
    for c in range(TOKENS // CHUNK):
        count = score[1, :, c * CHUNK:(c + 1) * CHUNK]
        weight = jnp.where(count > 0.5, count * jnp.exp(score[0, :, c * CHUNK:(c + 1) * CHUNK] - m_local), 0.0)
        for b in range(CHUNK // 128):
            sums = sums + weight[:, b * 128:(b + 1) * 128]
        pages = CHUNK // PAGE
        o_local = o_local + dot(
            weight.astype(BF16), pool[c * pages:(c + 1) * pages, :, HD:2 * HD].reshape(CHUNK, HD)
        )
    l_local = jnp.sum(sums, axis=1, keepdims=True)
    key32 = jnp.concatenate([pair8[:, 0:HD]] * 4, axis=0)
    value32 = jnp.concatenate([pair8[:, HD:2 * HD]] * 4, axis=0)
    own_score = jnp.sum(q32 * key32, axis=1, keepdims=True) * SCALE

    await_all(PARTIAL, lambda peer: tx2.at[peer], rx2, me)
    back = rx2[...].astype(F32)
    m_s = back[:, :, HD:HD + 1]
    l_s = back[:, :, HD + 1:HD + 2] + back[:, :, HD + 2:HD + 3]
    m_r = jnp.max(m_s, axis=0)
    w_s = jnp.exp(m_s - m_r[None])
    l_r = jnp.sum(w_s * l_s, axis=0)
    o_r = jnp.sum(w_s * back[:, :, 0:HD], axis=0)
    at = iota((16, 128), 1)
    far = jnp.concatenate([o_r, jnp.where(at == 0, m_r, l_r)], axis=1)
    nothing = jnp.where(iota((4, 384), 1) == HD, NONE, 0.0)
    far = jnp.concatenate([x for h in range(4) for x in (nothing, far[4 * h:4 * h + 4])], axis=0)
    o_r, m_r, l_r = far[:, 0:HD], far[:, HD:HD + 1], far[:, HD + 1:HD + 2]
    top = jnp.maximum(jnp.maximum(m_local, m_r), own_score)
    f_local, f_far, f_own = jnp.exp(m_local - top), jnp.exp(m_r - top), jnp.exp(own_score - top)
    below = f_local * l_local + f_far * l_r + f_own
    above = f_local * o_local + f_far * o_r + f_own.astype(BF16).astype(F32) * value32
    attended = above / below
    attended = jnp.concatenate([attended[0:16], attended[16:32]], axis=1).astype(BF16)
    tx3[...] = attended
    rx3[me] = attended
    spread_attn(HEADS_OUT, lambda peer: tx3, rx3, me)
    l_wo.wait()
    await_all(HEADS_OUT, lambda peer: tx3, rx3, me)

    gathered = rx3[...].astype(F32)
    x = [gathered[:, 8 * i:8 * i + 8, :].reshape(128, 512).astype(BF16) for i in range(2)]
    partial = jnp.zeros((128, W), F32)
    for h in range(4):
        partial = partial + dot_nt(x[h % 2][:, (h // 2) * HD:(h // 2 + 1) * HD], wo[:, h * HD:(h + 1) * HD])

    def padded(rows):
        return jnp.concatenate([rows, jnp.zeros((rows.shape[0], 512 - W), F32)], axis=1)

    tx4[...] = fold(padded(partial).reshape(NG, 8, 512)).astype(BF16)
    rx4[g_me] = tx4[g_me]
    spread_group(PROJ, lambda peer: tx4.at[peer], rx4)

    l_resid.wait()
    l_gain.wait()
    owned = iota((8, 128), 0)
    owned = (owned // 4) * 64 + g_me * 4 + owned % 4 == iota((8, 128), 1)
    own_resid = padded(dot(jnp.where(owned, 1.0, 0.0).astype(BF16), resid_v[...].reshape(128, W)))
    gain = padded(gain_v[...].astype(F32).reshape(1, W))
    await_all(PROJ, lambda peer: tx4.at[peer], rx4, g_me)
    hidden = own_resid + unfold(jnp.sum(rx4[...].astype(F32), axis=0))
    hidden_v[...] = hidden
    squares = jnp.sum(hidden * hidden, axis=1, keepdims=True)
    high = squares.astype(BF16).astype(F32)
    scaled = hidden * gain
    scaled = jnp.where(edge_lane == W, high, jnp.where(edge_lane == W + 1, squares - high, scaled))
    scaled = fold(scaled).astype(BF16)
    tx5[...] = scaled
    rx5[g_me] = scaled
    spread_group(ROWS_IN, lambda peer: tx5, rx5)
    await_all(ROWS_IN, lambda peer: tx5, rx5, g_me)

    rows = unfold(rx5[...].astype(F32)).reshape(128, 512).astype(BF16)
    rows_v[...] = rows
    stats = dot_nt(edge[...], rows)
    tx6[...] = stats
    rx6[me] = stats
    spread_attn(STATS, lambda peer: tx6, rx6, me)
    slots_v[...] = dot(pick[0:2 * CAP, :].astype(BF16), rows_v[:, 0:W]).astype(BF16)

    l_wg.wait()
    l_wu.wait()
    left = iota((2 * CAP, 128), 1) < 64

    for p in range(4):
        slots = slots_v[...]
        g = dot(slots, wg[:, 640 * p:640 * p + 640])
        u = dot(slots, wu[:, 640 * p:640 * p + 640])
        g2, u2 = g[:, 256:384], pltpu.roll(u[:, 256:384], 64, axis=1)
        pieces = (
            (g[:, 0:256], u[:, 0:256], jnp.where(left, g2, u2)),
            (g[:, 384:640], u[:, 384:640], jnp.where(left, u2, g2)),
        )
        for i in range(2):
            piece = jnp.concatenate(pieces[i], axis=1)
            j = 2 * p + i
            own_v[j] = piece[0:CAP]
            txs[j] = piece[CAP:2 * CAP].astype(BF16)
            remote(SIBLING, txs.at[j], rxs.at[j], j, j, attn_id(sibling)).start()

    def reduce_piece(i, _):
        j = lax.rem(chip + 1 + i, CHIPS)
        remote(SIBLING, txs.at[j], rxs.at[j], j, j, attn_id(sibling)).wait_recv()
        tx7[j] = (own_v[j] + rxs[j].astype(F32)).astype(BF16)

        @pl.when(i < CHIPS - 1)
        def _():
            remote(REDUCE, tx7.at[j], rx7.at[chip], j, chip, attn_id(2 * j + core)).start()

        return 0

    lax.fori_loop(0, CHIPS, reduce_piece, 0)
    rx7[chip] = tx7[chip]

    await_all(STATS, lambda peer: tx6, rx6, me)
    stats = jnp.sum(rx6[...], axis=0)
    inverse_row = lax.rsqrt(stats[1:2] / D + EPSILON)
    route_row = 1.0 / (1.0 + jnp.exp(-(stats[0:1] * inverse_row)))
    picked = pick[0:2 * CAP, :]
    inverse = jnp.sum(picked[0:CAP] * inverse_row, axis=1, keepdims=True)
    route = jnp.sum(picked * route_row, axis=1, keepdims=True)

    def await_piece(i, _):
        j = lax.rem(chip + i, CHIPS)
        remote(REDUCE, tx7.at[j], rx7.at[j], j, j, attn_id(me)).wait_recv()
        return 0

    lax.fori_loop(1, CHIPS, await_piece, 0)
    total = rx7[0].astype(F32)
    for j in range(1, CHIPS):
        total = total + rx7[j].astype(F32)
    total = total * inverse
    mixed = total[:, 512:640]
    half = silu(mixed) * pltpu.roll(mixed, 64, axis=1)
    right = jnp.where(iota((CAP, 128), 1) < 64, 0, 1)
    half = jnp.where(right == lax.rem(chip, 2), half, 0.0)
    activated = jnp.concatenate([silu(total[:, 0:256]) * total[:, 256:512], half], axis=1).astype(BF16)
    tx8[...] = activated
    rx8[0, chip] = activated
    remote(FORWARD, tx8, rx8.at[1, chip], chip, chip, attn_id(sibling)).start()

    def send_act(i, _):
        j = lax.rem(chip + i, CHIPS)
        remote(ACT, tx8, rx8.at[0, chip], j, chip, attn_id(2 * j + core)).start()
        return 0

    lax.fori_loop(1, CHIPS, send_act, 0)

    def forward(i, _):
        j = lax.rem(chip + i, CHIPS)
        remote(ACT, tx8, rx8.at[0, j], j, j, attn_id(me)).wait_recv()
        remote(FORWARD, rx8.at[0, j], rx8.at[1, j], j, j, attn_id(sibling)).start()
        return 0

    lax.fori_loop(1, CHIPS, forward, 0)
    l_wd.wait()

    def await_forward(i, _):
        remote(FORWARD, tx8, rx8.at[1, i], i, i, attn_id(me)).wait_recv()
        return 0

    lax.fori_loop(0, CHIPS, await_forward, 0)
    result = jnp.zeros((2 * CAP, W), F32)
    for p in range(4):
        parts = []
        for side in range(2):
            a, b = rx8[side, 2 * p], rx8[side, 2 * p + 1]
            middle = (a[:, 256:384].astype(F32) + b[:, 256:384].astype(F32)).astype(BF16)
            parts.append(jnp.concatenate([a[:, 0:256], middle, b[:, 0:256]], axis=1))
        result = result + dot_nt(jnp.concatenate(parts, axis=0), wd[:, 640 * p:640 * p + 640])
    result = (result * route).astype(BF16)
    added = dot(spread[:, 0:2 * CAP], result)
    tx9[...] = fold(padded(added).reshape(NG, 8, 512)).astype(BF16)
    rx9[g_me] = tx9[g_me]
    spread_group(BACK, lambda peer: tx9.at[peer], rx9)
    await_all(BACK, lambda peer: tx9.at[peer], rx9, g_me)
    final = hidden_v[...] + unfold(jnp.sum(rx9[...].astype(F32), axis=0))
    out[0] = final[0:4, 0:W].astype(BF16)
    out[1] = final[4:8, 0:W].astype(BF16)

    def done(i, _):
        peer = lax.rem(me + i, NA)
        for phase, src, dst in (
            (QUERY, tx1.at[peer], rx1.at[peer]), (PARTIAL, tx2.at[peer], rx2.at[peer]), (HEADS_OUT, tx3, rx3.at[peer]),
            (STATS, tx6, rx6.at[peer]),
        ):
            remote(phase, src, dst, peer, peer, attn_id(me)).wait_send()
        peer = lax.rem(g_me + i, NG)
        for phase, src, dst in (
            (PROJ, tx4.at[peer], rx4.at[peer]), (ROWS_IN, tx5, rx5.at[peer]), (BACK, tx9.at[peer], rx9.at[peer]),
        ):
            remote(phase, src, dst, peer, peer, attn_id(me)).wait_send()
        return 0

    lax.fori_loop(1, NA, done, 0)

    def done_pieces(j, _):
        remote(SIBLING, txs.at[j], rxs.at[j], j, j, attn_id(me)).wait_send()
        remote(FORWARD, tx8, rx8.at[1, j], j, j, attn_id(me)).wait_send()

        @pl.when(j != chip)
        def _():
            remote(REDUCE, tx7.at[j], rx7.at[j], j, j, attn_id(me)).wait_send()
            remote(ACT, tx8, rx8.at[0, j], j, j, attn_id(me)).wait_send()

        return 0

    lax.fori_loop(0, CHIPS, done_pieces, 0)


def on_device(
    queries, new_pairs, kv_pool, table_first, table_second, lengths, migrations, residual,
    out_proj, norm_gain, router, routes, gate_weight, up_weight, down_weight,
):
    vmem, smem = pltpu.VMEM, pltpu.SMEM
    return pl.pallas_call(
        body,
        out_shape=jax.ShapeDtypeStruct((2, 4, W), BF16),
        in_specs=[pl.BlockSpec(memory_space=pltpu.HBM)] * 15,
        out_specs=pl.BlockSpec(memory_space=pltpu.VMEM),
        scratch_shapes=[
            smem((2, 4), jnp.int32), smem((1, 16), jnp.int32),
            vmem((2, 4, 1024), BF16), vmem((2, 4, 512), BF16), vmem((LOCAL, PAGE, 2 * HD), BF16),
            vmem((4, 16), jnp.int32), vmem((4, 16), jnp.int32), vmem((2, 64, W), BF16), vmem((W, 1024), BF16),
            vmem((W,), BF16), vmem((1, W), BF16), vmem((3, 2, 64), jnp.int32),
            vmem((W, 2560), BF16), vmem((W, 2560), BF16), vmem((W, 2560), BF16),
            pltpu.SemaphoreType.DMA((15,)), pltpu.SemaphoreType.DMA((11, 16)), pltpu.SemaphoreType.DMA((11, 16)),
            vmem((NA, 16, 384), BF16), vmem((NA, 16, 384), BF16),
            vmem((NA, 16, 384), BF16), vmem((NA, 16, 384), BF16),
            vmem((16, 512), BF16), vmem((NA, 16, 512), BF16),
            vmem((NG, 16, 256), BF16), vmem((NG, 16, 256), BF16),
            vmem((16, 256), BF16), vmem((NG, 16, 256), BF16),
            vmem((8, 128), F32), vmem((NA, 8, 128), F32),
            vmem((CHIPS, CAP, 640), BF16), vmem((CHIPS, CAP, 640), BF16),
            vmem((CHIPS, CAP, 640), BF16), vmem((CHIPS, CAP, 640), BF16),
            vmem((CAP, 384), BF16), vmem((2, CHIPS, CAP, 384), BF16),
            vmem((NG, 16, 256), BF16), vmem((NG, 16, 256), BF16),
            vmem((2, 32, TOKENS), F32), vmem((8, 512), F32), vmem((2 * CAP, W), BF16), vmem((128, 512), BF16),
            vmem((128, 128), F32), vmem((128, 128), BF16), vmem((8, 512), BF16), vmem((CHIPS, CAP, 640), F32),
        ],
        compiler_params=pltpu.CompilerParams(
            collective_id=0, has_side_effects=True, vmem_limit_bytes=60 * 1024 * 1024
        ),
        name="layer",
    )(
        queries, new_pairs, kv_pool, table_first, table_second, lengths, migrations, residual,
        out_proj.T, norm_gain, router.T, routes.transpose(2, 0, 1), gate_weight, up_weight, down_weight[0].T,
    )


def solution(mesh):
    return jax.shard_map(
        on_device,
        mesh=mesh,
        in_specs=(
            P(None, "attn", ("ffn", "tp")),
            P(None, "attn", None),
            P("attn", None, None),
            P("attn", None),
            P("attn", None),
            P(None, "attn"),
            P("attn", None),
            P(None, None, "attn"),
            P(("ffn", "tp"), "attn"),
            P("attn"),
            P("attn", "ffn"),
            P(),
            P("ffn", "attn", "tp"),
            P("ffn", "attn", "tp"),
            P("ffn", "tp", "attn"),
        ),
        out_specs=P(None, ("ffn", "tp"), "attn"),
        check_vma=False,
    )
```

```python
import jax
import jax.numpy as jnp
from jax import lax
from jax.experimental import pallas as pl
from jax.experimental.pallas import tpu as pltpu
from jax.sharding import PartitionSpec as P

F32, BF16 = jnp.float32, jnp.bfloat16
MESH = pl.DeviceIdType.MESH
D = 7168
EPSILON = 1e-6
NA, NG = 16, 16
CHIPS = 8
LOCAL = 48
PAGE, HD = 64, 256
TOKENS = LOCAL * PAGE
CHUNK = 512
CAP = 48
W = 448
NONE = -1e30
SCALE = HD ** -0.5
NT_DIMS = (((1,), (1,)), ((), ()))
ATTN_ORDER = [(dx, dy, dc) for dx in (2, 1, 3, 0) for dy in (1, 0) for dc in (0, 1) if (dx, dy, dc) != (0, 0, 0)]
GROUP_ORDER = [(dz, dt) for dz in (4, 3, 5, 2, 6, 1, 7, 0) for dt in (1, 0) if (dz, dt) != (0, 0)]
NEIGHBOURS = [(1, 1), (7, 1), (0, 1), (1, 0), (7, 0)]
NEAR_FIRST = (0, 1, 3, 2)
QUERY, PARTIAL, HEADS_OUT, PROJ, ROWS_IN, STATS, SIBLING, REDUCE, ACT, FORWARD, BACK = range(11)
TOGETHER = (PARTIAL, HEADS_OUT, PROJ, ROWS_IN, STATS, BACK)


def iota(shape, axis):
    return lax.broadcasted_iota(jnp.int32, shape, axis)


def dot(a, b):
    return jnp.dot(a, b, preferred_element_type=F32)


def dot_nt(a, b):
    return lax.dot_general(a, b, NT_DIMS, preferred_element_type=F32)


def fold(block):
    return jnp.concatenate([block[..., :256], block[..., 256:]], axis=-2)


def unfold(block):
    return jnp.concatenate([block[..., :8, :], block[..., 8:, :]], axis=-1)


def silu(v):
    return v / (1.0 + jnp.exp(-v))


def body(
    queries, new_pairs, kv_pool, table_first, table_second, lengths_in, migrations_in, residual,
    out_proj, norm_gain, router, routes, gate_weight, up_weight, down_weight,
    out,
    lengths, migrations, q_v, pair_v, pool, tab1, tab2, resid_v, wo, gain_v, router_v, routes_v, wg, wu, wd,
    load_sem, send, recv, gossip,
    tx1, rx1, tx2, rx2, tx3, rx3, tx4, rx4, tx5, rx5, tx6, rx6, txs, rxs, tx7, rx7, tx8, rx8, tx9, rx9,
    score, base_v, hidden_v, slots_v, rows_v, pick, spread, edge, own_v,
):
    me = lax.axis_index("attn")
    expert = lax.axis_index("ffn")
    g_me = expert * 2 + lax.axis_index("tp")
    core = lax.rem(me, 2)
    chip = me // 2
    sibling = me + 1 - 2 * core
    at_x, at_y = me // 4, lax.rem(chip, 2)
    at_t = lax.rem(g_me, 2)

    def attn_peer(dx, dy, dc):
        return lax.rem(at_x + dx, 4) * 4 + lax.rem(at_y + dy, 2) * 2 + lax.rem(core + dc, 2)

    def chip_peer(dx, dy):
        return lax.rem(at_x + dx, 4) * 2 + lax.rem(at_y + dy, 2)

    def group_peer(dz, dt):
        return lax.rem(expert + dz, 8) * 2 + lax.rem(at_t + dt, 2)

    pairs = [
        (queries, q_v), (table_second, tab2), (table_first, tab1), (new_pairs, pair_v),
        (lengths_in, lengths), (migrations_in, migrations),
        (kv_pool.at[pl.ds(0, LOCAL)], pool), (routes, routes_v), (router, router_v), (norm_gain, gain_v),
        (residual, resid_v), (out_proj, wo), (gate_weight.at[0], wg), (up_weight.at[0], wu), (down_weight, wd),
    ]
    loads = [pltpu.make_async_copy(src, dst, load_sem.at[i]) for i, (src, dst) in enumerate(pairs)]
    for load in loads:
        load.start()
    (l_q, l_t2, l_t1, l_pair, l_len, l_mig, l_pool, l_routes, l_router, l_gain, l_resid, l_wo, l_wg, l_wu, l_wd) = loads

    def attn_id(i):
        return {"attn": i}

    def group_id(g):
        return {"ffn": g // 2, "tp": lax.rem(g, 2)}

    barrier = pltpu.get_barrier_semaphore()

    for step in ATTN_ORDER:
        pl.semaphore_signal(barrier, inc=1, device_id=attn_id(attn_peer(*step)), device_id_type=MESH)
    for step in NEIGHBOURS:
        pl.semaphore_signal(barrier, inc=1, device_id=group_id(group_peer(*step)), device_id_type=MESH)

    def tell(i):
        for dz in (1, 7):
            pl.semaphore_signal(gossip.at[i], inc=1, device_id=group_id(group_peer(dz, 0)), device_id_type=MESH)

    def hear(i):
        pl.semaphore_wait(gossip.at[i], 2)

    def remote(phase, src, dst, slot_to, slot_from, device):
        return pltpu.make_async_remote_copy(
            src_ref=src, dst_ref=dst, send_sem=send.at[phase], recv_sem=recv.at[phase, 0 if phase in TOGETHER else slot_from],
            device_id=device, device_id_type=MESH,
        )

    l_q.wait()
    l_t2.wait()
    l_len.wait()
    q8 = jnp.concatenate([q_v[0].astype(F32), q_v[1].astype(F32)], axis=0)
    t2 = tab2[...]
    t2x = jnp.concatenate([t2, t2, t2, t2], axis=0)

    def column(rows, values):
        at = iota((rows, 1), 0)
        result = jnp.zeros((rows, 1), jnp.int32)
        for i in range(rows):
            result = jnp.where(at == i, values[i], result)
        return result

    len2 = column(16, [lengths[1, i % 4] for i in range(16)])
    len8 = column(8, [lengths[i // 4, i % 4] for i in range(8)])

    def counts(table, length, first, width):
        lane = iota((table.shape[0], width), 1)
        page, place = first + lane // PAGE, lane % PAGE
        total = jnp.zeros((table.shape[0], width), F32)
        for k in range(16):
            left = length - k * PAGE
            total = total + jnp.where((page == table[:, k:k + 1]) & (place < left), 1.0, 0.0)
        return total

    q2 = jnp.concatenate([q8[4:8, h * HD:(h + 1) * HD] for h in range(4)], axis=0).astype(BF16)
    for s in range(0, NA, 2):
        c = counts(t2x, len2, LOCAL + s, 2 * PAGE)
        tx1[s, :, 0:HD] = q2
        tx1[s, :, HD:384] = c.astype(BF16)
        tx1[s + 1, :, 0:HD] = q2
        tx1[s + 1, :, HD:384] = pltpu.roll(c, PAGE, axis=1).astype(BF16)
    rx1[me] = tx1[me]

    l_routes.wait()
    l_router.wait()
    named = [routes_v[i] == expert for i in range(3)]
    chosen = jnp.where(named[0] | named[1] | named[2], 1.0, 0.0)
    chosen = jnp.concatenate([chosen[0:1], chosen[1:2]], axis=1)
    row, lane = iota((128, 128), 0), iota((128, 128), 1)
    row_step = (row % 8) // 4
    natural = row_step * 64 + (row // 8) * 4 + row % 4
    chosen_at = jnp.sum(jnp.where(lane == natural, chosen, 0.0), axis=1, keepdims=True)
    before = (lane < natural) & (lane // 64 == row_step)
    rank = jnp.sum(jnp.where(before, chosen, 0.0), axis=1, keepdims=True).astype(jnp.int32)
    slot_at = rank + jnp.where(row_step == core, 0, CAP)
    picked = jnp.where((lane == slot_at) & (chosen_at > 0.5), 1.0, 0.0)
    spread[...] = picked.astype(BF16)
    pick[...] = jnp.transpose(picked)
    router_row = jnp.concatenate([router_v[...].astype(F32), jnp.zeros((1, 512 - W), F32)], axis=1)
    edge_row, edge_lane = iota((8, 512), 0), iota((8, 512), 1)
    edge[...] = jnp.where(
        edge_row == 0, router_row, jnp.where((edge_row == 1) & (edge_lane >= W) & (edge_lane < W + 2), 1.0, 0.0)
    ).astype(BF16)

    def padded(rows):
        return jnp.concatenate([rows, jnp.zeros((rows.shape[0], 512 - W), F32)], axis=1)

    l_resid.wait()
    l_gain.wait()
    owned = iota((8, 128), 0)
    owned = (owned // 4) * 64 + g_me * 4 + owned % 4 == iota((8, 128), 1)
    base_v[0:8] = padded(dot(jnp.where(owned, 1.0, 0.0).astype(BF16), resid_v[...].reshape(128, W)))
    base_v[8:16] = jnp.broadcast_to(padded(gain_v[...].astype(F32).reshape(1, W)), (8, 512))

    pl.semaphore_wait(barrier, len(ATTN_ORDER) + len(NEIGHBOURS))

    def spread_attn(phase, src_of, dst, slot):
        for step in ATTN_ORDER:
            peer = attn_peer(*step)
            remote(phase, src_of(peer), dst.at[slot], peer, slot, attn_id(peer)).start()

    def spread_group(phase, src_of, dst):
        for step in GROUP_ORDER:
            peer = group_peer(*step)
            remote(phase, src_of(peer), dst.at[g_me], peer, g_me, group_id(peer)).start()

    def await_all(phase, dst):
        every = dst.at[pl.ds(0, 15)]
        remote(phase, every, every, 0, 0, attn_id(me)).wait_recv()

    spread_attn(QUERY, lambda peer: tx1.at[peer], rx1, me)
    tell(0)

    l_pool.wait()
    l_mig.wait()
    l_t1.wait()
    l_pair.wait()
    t8 = jnp.concatenate([tab1[...], t2], axis=0)
    q32 = jnp.concatenate([q8[:, h * HD:(h + 1) * HD] for h in range(4)], axis=0)
    q32b = q32.astype(BF16)
    pair8 = jnp.concatenate([pair_v[0].astype(F32), pair_v[1].astype(F32)], axis=0)
    peak = jnp.full((32, 128), NONE, F32)
    all_counts = []
    for c in range(TOKENS // CHUNK):
        pages = CHUNK // PAGE
        count = counts(t8, len8, c * pages, CHUNK)
        count = jnp.concatenate([count] * 4, axis=0)
        s = dot_nt(q32b, pool[c * pages:(c + 1) * pages, :, 0:HD].reshape(CHUNK, HD)) * SCALE
        s = jnp.where(count > 0.5, s, NONE)
        score[0, :, c * CHUNK:(c + 1) * CHUNK] = s
        score[1, :, c * CHUNK:(c + 1) * CHUNK] = count
        for b in range(CHUNK // 128):
            peak = jnp.maximum(peak, s[:, b * 128:(b + 1) * 128])
    m_local = jnp.max(peak, axis=1, keepdims=True)
    sums = jnp.zeros((32, 128), F32)
    o_local = jnp.zeros((32, HD), F32)
    for c in range(TOKENS // CHUNK):
        count = score[1, :, c * CHUNK:(c + 1) * CHUNK]
        weight = jnp.where(count > 0.5, count * jnp.exp(score[0, :, c * CHUNK:(c + 1) * CHUNK] - m_local), 0.0)
        for b in range(CHUNK // 128):
            sums = sums + weight[:, b * 128:(b + 1) * 128]
        pages = CHUNK // PAGE
        o_local = o_local + dot(
            weight.astype(BF16), pool[c * pages:(c + 1) * pages, :, HD:2 * HD].reshape(CHUNK, HD)
        )
    l_local = jnp.sum(sums, axis=1, keepdims=True)
    key32 = jnp.concatenate([pair8[:, 0:HD]] * 4, axis=0)
    value32 = jnp.concatenate([pair8[:, HD:2 * HD]] * 4, axis=0)
    own_score = jnp.sum(q32 * key32, axis=1, keepdims=True) * SCALE

    for dx in NEAR_FIRST:
        steps = [(dx, dy, dc) for dy in (0, 1) for dc in (0, 1)]
        sources = [attn_peer(*step) for step in steps]
        for step, source in zip(steps, sources):
            if step != (0, 0, 0):
                remote(QUERY, tx1.at[source], rx1.at[source], source, source, attn_id(me)).wait_recv()
        pages = [migrations[0, source] for source in sources]
        asked = [rx1[source] for source in sources]
        count = jnp.concatenate([a[:, HD:HD + PAGE].astype(F32) for a in asked], axis=0)
        s = jnp.concatenate([dot_nt(a[:, 0:HD], pool[page, :, 0:HD]) for a, page in zip(asked, pages)], axis=0) * SCALE
        live = count > 0.5
        top = jnp.max(jnp.where(live, s, NONE), axis=1, keepdims=True).astype(BF16).astype(F32)
        weight = jnp.where(live, count * jnp.exp(s - top), 0.0)
        total = jnp.sum(weight, axis=1, keepdims=True)
        high = total.astype(BF16).astype(F32)
        at = iota((64, 128), 1)
        stat = jnp.where(at == 0, top, jnp.where(at == 1, high, jnp.where(at == 2, total - high, 0.0))).astype(BF16)
        weight = weight.astype(BF16)
        for i, (step, source) in enumerate(zip(steps, sources)):
            tx2[source, :, 0:HD] = dot(weight[16 * i:16 * i + 16], pool[pages[i], :, HD:2 * HD]).astype(BF16)
            tx2[source, :, HD:384] = stat[16 * i:16 * i + 16]
        for step, source in zip(steps, sources):
            if step != (0, 0, 0):
                remote(PARTIAL, tx2.at[source], rx2.at[me], source, me, attn_id(source)).start()
    rx2[me] = tx2[me]
    hear(0)
    tell(1)

    await_all(PARTIAL, rx2)
    back = rx2[...].astype(F32)
    m_s = back[:, :, HD:HD + 1]
    l_s = back[:, :, HD + 1:HD + 2] + back[:, :, HD + 2:HD + 3]
    m_r = jnp.max(m_s, axis=0)
    w_s = jnp.exp(m_s - m_r[None])
    l_r = jnp.sum(w_s * l_s, axis=0)
    o_r = jnp.sum(w_s * back[:, :, 0:HD], axis=0)
    at = iota((16, 128), 1)
    far = jnp.concatenate([o_r, jnp.where(at == 0, m_r, l_r)], axis=1)
    nothing = jnp.where(iota((4, 384), 1) == HD, NONE, 0.0)
    far = jnp.concatenate([x for h in range(4) for x in (nothing, far[4 * h:4 * h + 4])], axis=0)
    o_r, m_r, l_r = far[:, 0:HD], far[:, HD:HD + 1], far[:, HD + 1:HD + 2]
    top = jnp.maximum(jnp.maximum(m_local, m_r), own_score)
    f_local, f_far, f_own = jnp.exp(m_local - top), jnp.exp(m_r - top), jnp.exp(own_score - top)
    below = f_local * l_local + f_far * l_r + f_own
    above = f_local * o_local + f_far * o_r + f_own.astype(BF16).astype(F32) * value32
    attended = above / below
    attended = jnp.concatenate([attended[0:16], attended[16:32]], axis=1).astype(BF16)
    tx3[...] = attended
    rx3[me] = attended
    spread_attn(HEADS_OUT, lambda peer: tx3, rx3, me)
    hear(1)
    tell(2)
    l_wo.wait()
    await_all(HEADS_OUT, rx3)

    gathered = rx3[...].astype(F32)
    x = [gathered[:, 8 * i:8 * i + 8, :].reshape(128, 512).astype(BF16) for i in range(2)]
    partial = jnp.zeros((128, W), F32)
    for h in range(4):
        partial = partial + dot_nt(x[h % 2][:, (h // 2) * HD:(h // 2 + 1) * HD], wo[:, h * HD:(h + 1) * HD])

    tx4[...] = fold(padded(partial).reshape(NG, 8, 512)).astype(BF16)
    rx4[g_me] = tx4[g_me]
    hear(2)
    spread_group(PROJ, lambda peer: tx4.at[peer], rx4)

    await_all(PROJ, rx4)
    hidden = base_v[0:8] + unfold(jnp.sum(rx4[...].astype(F32), axis=0))
    hidden_v[...] = hidden
    squares = jnp.sum(hidden * hidden, axis=1, keepdims=True)
    high = squares.astype(BF16).astype(F32)
    scaled = hidden * base_v[8:16]
    scaled = jnp.where(edge_lane == W, high, jnp.where(edge_lane == W + 1, squares - high, scaled))
    scaled = fold(scaled).astype(BF16)
    tx5[...] = scaled
    rx5[g_me] = scaled
    spread_group(ROWS_IN, lambda peer: tx5, rx5)
    await_all(ROWS_IN, rx5)

    rows = unfold(rx5[...].astype(F32)).reshape(128, 512).astype(BF16)
    rows_v[...] = rows
    stats = dot_nt(edge[...], rows)
    tx6[...] = stats
    rx6[me] = stats
    spread_attn(STATS, lambda peer: tx6, rx6, me)
    slots_v[...] = dot(pick[0:2 * CAP, :].astype(BF16), rows_v[:, 0:W]).astype(BF16)

    l_wg.wait()
    l_wu.wait()
    left = iota((2 * CAP, 128), 1) < 64

    def compute_pair(p):
        lanes = pl.ds(pl.multiple_of(640 * p, 128), 640)
        g = dot(slots_v[...], wg[:, lanes])
        u = dot(slots_v[...], wu[:, lanes])
        g2, u2 = g[:, 256:384], pltpu.roll(u[:, 256:384], 64, axis=1)
        pieces = (
            (g[:, 0:256], u[:, 0:256], jnp.where(left, g2, u2)),
            (g[:, 384:640], u[:, 384:640], jnp.where(left, u2, g2)),
        )
        for i in range(2):
            piece = jnp.concatenate(pieces[i], axis=1)
            j = 2 * p + i
            own_v[j] = piece[0:CAP]
            txs[j] = piece[CAP:2 * CAP].astype(BF16)
            remote(SIBLING, txs.at[j], rxs.at[j], j, j, attn_id(sibling)).start()

    def reduce_pair(dx):
        for dy in (1, 0):
            j = chip_peer(dx, dy)
            remote(SIBLING, txs.at[j], rxs.at[j], j, j, attn_id(sibling)).wait_recv()
            tx7[j] = (own_v[j] + rxs[j].astype(F32)).astype(BF16)
            if (dx, dy) != (0, 0):
                remote(REDUCE, tx7.at[j], rx7.at[chip], j, chip, attn_id(2 * j + core)).start()

    far_first = (2, 1, 3, 0)
    for k, dx in enumerate(far_first):
        compute_pair(lax.rem(at_x + dx, 4))
        if k > 0:
            reduce_pair(far_first[k - 1])
    reduce_pair(0)

    await_all(STATS, rx6)
    stats = jnp.sum(rx6[...], axis=0)
    inverse_row = lax.rsqrt(stats[1:2] / D + EPSILON)
    route_row = 1.0 / (1.0 + jnp.exp(-(stats[0:1] * inverse_row)))
    picked = pick[0:2 * CAP, :]
    inverse = jnp.sum(picked[0:CAP] * inverse_row, axis=1, keepdims=True)
    route = jnp.sum(picked * route_row, axis=1, keepdims=True)

    total = tx7[chip].astype(F32)
    for dx in NEAR_FIRST:
        for dy in (0, 1):
            if (dx, dy) != (0, 0):
                j = chip_peer(dx, dy)
                remote(REDUCE, tx7.at[j], rx7.at[j], j, j, attn_id(me)).wait_recv()
                total = total + rx7[j].astype(F32)
    total = total * inverse
    mixed = total[:, 512:640]
    half = silu(mixed) * pltpu.roll(mixed, 64, axis=1)
    right = jnp.where(iota((CAP, 128), 1) < 64, 0, 1)
    half = jnp.where(right == lax.rem(chip, 2), half, 0.0)
    activated = jnp.concatenate([silu(total[:, 0:256]) * total[:, 256:512], half], axis=1).astype(BF16)
    tx8[...] = activated
    rx8[0, chip] = activated
    for dx in far_first:
        for dy in (1, 0):
            if (dx, dy) != (0, 0):
                j = chip_peer(dx, dy)
                remote(ACT, tx8, rx8.at[0, chip], j, chip, attn_id(2 * j + core)).start()
    remote(FORWARD, tx8, rx8.at[1, chip], chip, chip, attn_id(sibling)).start()
    l_wd.wait()

    def forward_pair(dx):
        for dy in (0, 1):
            if (dx, dy) != (0, 0):
                j = chip_peer(dx, dy)
                remote(ACT, tx8, rx8.at[0, j], j, j, attn_id(me)).wait_recv()
                remote(FORWARD, rx8.at[0, j], rx8.at[1, j], j, j, attn_id(sibling)).start()

    def down_pair(dx):
        p = lax.rem(at_x + dx, 4)
        for j in (2 * p, 2 * p + 1):
            remote(FORWARD, tx8, rx8.at[1, j], j, j, attn_id(me)).wait_recv()
        parts = []
        for side in range(2):
            a, b = rx8[side, 2 * p], rx8[side, 2 * p + 1]
            middle = (a[:, 256:384].astype(F32) + b[:, 256:384].astype(F32)).astype(BF16)
            parts.append(jnp.concatenate([a[:, 0:256], middle, b[:, 0:256]], axis=1))
        lanes = pl.ds(pl.multiple_of(640 * p, 128), 640)
        return dot_nt(jnp.concatenate(parts, axis=0), wd[:, lanes])

    result = jnp.zeros((2 * CAP, W), F32)
    for k, dx in enumerate(NEAR_FIRST):
        forward_pair(dx)
        if k > 0:
            result = result + down_pair(NEAR_FIRST[k - 1])
    result = result + down_pair(NEAR_FIRST[3])
    result = (result * route).astype(BF16)
    added = dot(spread[:, 0:2 * CAP], result)
    tx9[...] = fold(padded(added).reshape(NG, 8, 512)).astype(BF16)
    rx9[g_me] = tx9[g_me]
    spread_group(BACK, lambda peer: tx9.at[peer], rx9)

    def sent(phase, every):
        remote(phase, every, every, 0, 0, attn_id(me)).wait_send()

    for phase, dst in ((QUERY, rx1), (PARTIAL, rx2), (HEADS_OUT, rx3), (PROJ, rx4), (ROWS_IN, rx5), (STATS, rx6), (BACK, rx9)):
        sent(phase, dst.at[pl.ds(0, 15)])
    sent(SIBLING, txs)
    sent(REDUCE, tx7.at[pl.ds(0, CHIPS - 1)])
    sent(ACT, rx8.at[0, pl.ds(0, CHIPS - 1)])
    sent(FORWARD, rx8.at[0])
    await_all(BACK, rx9)
    final = hidden_v[...] + unfold(jnp.sum(rx9[...].astype(F32), axis=0))
    out[0] = final[0:4, 0:W].astype(BF16)
    out[1] = final[4:8, 0:W].astype(BF16)


def on_device(
    queries, new_pairs, kv_pool, table_first, table_second, lengths, migrations, residual,
    out_proj, norm_gain, router, routes, gate_weight, up_weight, down_weight,
):
    vmem, smem = pltpu.VMEM, pltpu.SMEM
    return pl.pallas_call(
        body,
        out_shape=jax.ShapeDtypeStruct((2, 4, W), BF16),
        in_specs=[pl.BlockSpec(memory_space=pltpu.HBM)] * 15,
        out_specs=pl.BlockSpec(memory_space=pltpu.VMEM),
        scratch_shapes=[
            smem((2, 4), jnp.int32), smem((1, 16), jnp.int32),
            vmem((2, 4, 1024), BF16), vmem((2, 4, 512), BF16), vmem((LOCAL, PAGE, 2 * HD), BF16),
            vmem((4, 16), jnp.int32), vmem((4, 16), jnp.int32), vmem((2, 64, W), BF16), vmem((W, 1024), BF16),
            vmem((W,), BF16), vmem((1, W), BF16), vmem((3, 2, 64), jnp.int32),
            vmem((W, 2560), BF16), vmem((W, 2560), BF16), vmem((W, 2560), BF16),
            pltpu.SemaphoreType.DMA((15,)), pltpu.SemaphoreType.DMA((11,)), pltpu.SemaphoreType.DMA((11, 16)), pltpu.SemaphoreType.REGULAR((3,)),
            vmem((NA, 16, 384), BF16), vmem((NA, 16, 384), BF16),
            vmem((NA, 16, 384), BF16), vmem((NA, 16, 384), BF16),
            vmem((16, 512), BF16), vmem((NA, 16, 512), BF16),
            vmem((NG, 16, 256), BF16), vmem((NG, 16, 256), BF16),
            vmem((16, 256), BF16), vmem((NG, 16, 256), BF16),
            vmem((8, 128), F32), vmem((NA, 8, 128), F32),
            vmem((CHIPS, CAP, 640), BF16), vmem((CHIPS, CAP, 640), BF16),
            vmem((CHIPS, CAP, 640), BF16), vmem((CHIPS, CAP, 640), BF16),
            vmem((CAP, 384), BF16), vmem((2, CHIPS, CAP, 384), BF16),
            vmem((NG, 16, 256), BF16), vmem((NG, 16, 256), BF16),
            vmem((2, 32, TOKENS), F32), vmem((16, 512), F32), vmem((8, 512), F32), vmem((2 * CAP, W), BF16), vmem((128, 512), BF16),
            vmem((128, 128), F32), vmem((128, 128), BF16), vmem((8, 512), BF16), vmem((CHIPS, CAP, 640), F32),
        ],
        compiler_params=pltpu.CompilerParams(
            collective_id=0, has_side_effects=True, vmem_limit_bytes=60 * 1024 * 1024
        ),
        name="layer",
    )(
        queries, new_pairs, kv_pool, table_first, table_second, lengths, migrations, residual,
        out_proj.T, norm_gain, router.T, routes.transpose(2, 0, 1), gate_weight, up_weight, down_weight[0].T,
    )


def solution(mesh):
    return jax.shard_map(
        on_device,
        mesh=mesh,
        in_specs=(
            P(None, "attn", ("ffn", "tp")),
            P(None, "attn", None),
            P("attn", None, None),
            P("attn", None),
            P("attn", None),
            P(None, "attn"),
            P("attn", None),
            P(None, None, "attn"),
            P(("ffn", "tp"), "attn"),
            P("attn"),
            P("attn", "ffn"),
            P(),
            P("ffn", "attn", "tp"),
            P("ffn", "attn", "tp"),
            P("ffn", "tp", "attn"),
        ),
        out_specs=P(None, ("ffn", "tp"), "attn"),
        check_vma=False,
    )
```

```python
import jax
import jax.numpy as jnp
from jax import lax
from jax.experimental import pallas as pl
from jax.experimental.pallas import tpu as pltpu
from jax.sharding import PartitionSpec as P

F32, BF16 = jnp.float32, jnp.bfloat16
MESH = pl.DeviceIdType.MESH
D = 7168
EPSILON = 1e-6
NA, NG = 16, 16
CHIPS = 8
LOCAL = 48
PAGE, HD = 64, 256
TOKENS = LOCAL * PAGE
CHUNK = 512
CAP = 48
W = 448
NONE = -1e30
SCALE = HD ** -0.5
NT_DIMS = (((1,), (1,)), ((), ()))
ATTN_ORDER = [(dx, dy, dc) for dx in (2, 1, 3, 0) for dy in (1, 0) for dc in (0, 1) if (dx, dy, dc) != (0, 0, 0)]
GROUP_ORDER = [(dz, dt) for dt in (1, 0) for dz in (4, 3, 5, 2, 6, 1, 7, 0) if (dz, dt) != (0, 0)]
NEIGHBOURS = [(0, 1), (1, 0), (7, 0)]
NEAR_FIRST = (0, 1, 3, 2)
QUERY, PARTIAL, HEADS_OUT, PROJ, ROWS_IN, STATS, SIBLING, REDUCE, ACT, FORWARD, BACK, HEADS_FIRST = range(12)
TOGETHER = (PARTIAL, HEADS_OUT, PROJ, ROWS_IN, STATS, BACK, HEADS_FIRST)


def iota(shape, axis):
    return lax.broadcasted_iota(jnp.int32, shape, axis)


def dot(a, b):
    return jnp.dot(a, b, preferred_element_type=F32)


def dot_nt(a, b):
    return lax.dot_general(a, b, NT_DIMS, preferred_element_type=F32)


def fold(block):
    return jnp.concatenate([block[..., :256], block[..., 256:]], axis=-2)


def unfold(block):
    return jnp.concatenate([block[..., :8, :], block[..., 8:, :]], axis=-1)


def silu(v):
    return v / (1.0 + jnp.exp(-v))


def body(
    queries, new_pairs, kv_pool, table_first, table_second, lengths_in, migrations_in, residual,
    out_proj, norm_gain, router, routes, gate_weight, up_weight, down_weight,
    out,
    lengths, migrations, q_v, pair_v, pool, tab1, tab2, resid_v, wo, gain_v, router_v, routes_v, wg, wu, wd,
    load_sem, send, recv, gossip,
    tx1, rx1, tx2, rx2, tx3, rx3, tx4, rx4, tx5, rx5, tx6, rx6, txs, rxs, tx7, rx7, tx8, rx8, tx9, rx9,
    score, base_v, hidden_v, slots_v, rows_v, pick, spread, edge, own_v,
):
    me = lax.axis_index("attn")
    expert = lax.axis_index("ffn")
    g_me = expert * 2 + lax.axis_index("tp")
    core = lax.rem(me, 2)
    chip = me // 2
    sibling = me + 1 - 2 * core
    at_x, at_y = me // 4, lax.rem(chip, 2)
    at_t = lax.rem(g_me, 2)

    def attn_peer(dx, dy, dc):
        return lax.rem(at_x + dx, 4) * 4 + lax.rem(at_y + dy, 2) * 2 + lax.rem(core + dc, 2)

    def chip_peer(dx, dy):
        return lax.rem(at_x + dx, 4) * 2 + lax.rem(at_y + dy, 2)

    def group_peer(dz, dt):
        return lax.rem(expert + dz, 8) * 2 + lax.rem(at_t + dt, 2)

    pairs = [
        (queries, q_v), (table_second, tab2), (table_first, tab1), (new_pairs, pair_v),
        (lengths_in, lengths), (migrations_in, migrations),
        (kv_pool.at[pl.ds(0, LOCAL)], pool), (routes, routes_v), (router, router_v), (norm_gain, gain_v),
        (residual, resid_v), (out_proj, wo), (gate_weight.at[0], wg), (up_weight.at[0], wu), (down_weight, wd),
    ]
    loads = [pltpu.make_async_copy(src, dst, load_sem.at[i]) for i, (src, dst) in enumerate(pairs)]
    for load in loads:
        load.start()
    (l_q, l_t2, l_t1, l_pair, l_len, l_mig, l_pool, l_routes, l_router, l_gain, l_resid, l_wo, l_wg, l_wu, l_wd) = loads

    def attn_id(i):
        return {"attn": i}

    def group_id(g):
        return {"ffn": g // 2, "tp": lax.rem(g, 2)}

    barrier = pltpu.get_barrier_semaphore()

    for step in ATTN_ORDER:
        pl.semaphore_signal(barrier, inc=1, device_id=attn_id(attn_peer(*step)), device_id_type=MESH)
    for step in NEIGHBOURS:
        pl.semaphore_signal(barrier, inc=1, device_id=group_id(group_peer(*step)), device_id_type=MESH)

    def tell(i):
        for dz in (1, 7):
            pl.semaphore_signal(gossip.at[i], inc=1, device_id=group_id(group_peer(dz, 0)), device_id_type=MESH)

    def hear(i):
        pl.semaphore_wait(gossip.at[i], 2)

    def remote(phase, src, dst, slot_to, slot_from, device):
        return pltpu.make_async_remote_copy(
            src_ref=src, dst_ref=dst, send_sem=send.at[phase], recv_sem=recv.at[phase, 0 if phase in TOGETHER else slot_from],
            device_id=device, device_id_type=MESH,
        )

    l_q.wait()
    l_t2.wait()
    l_len.wait()
    q8 = jnp.concatenate([q_v[0].astype(F32), q_v[1].astype(F32)], axis=0)
    t2 = tab2[...]
    t2x = jnp.concatenate([t2, t2, t2, t2], axis=0)

    def column(rows, values):
        at = iota((rows, 1), 0)
        result = jnp.zeros((rows, 1), jnp.int32)
        for i in range(rows):
            result = jnp.where(at == i, values[i], result)
        return result

    len2 = column(16, [lengths[1, i % 4] for i in range(16)])
    len8 = column(8, [lengths[i // 4, i % 4] for i in range(8)])

    def counts(table, length, first, width):
        lane = iota((table.shape[0], width), 1)
        page, place = first + lane // PAGE, lane % PAGE
        total = jnp.zeros((table.shape[0], width), F32)
        for k in range(16):
            left = length - k * PAGE
            total = total + jnp.where((page == table[:, k:k + 1]) & (place < left), 1.0, 0.0)
        return total

    q2 = jnp.concatenate([q8[4:8, h * HD:(h + 1) * HD] for h in range(4)], axis=0).astype(BF16)
    for s in range(0, NA, 2):
        c = counts(t2x, len2, LOCAL + s, 2 * PAGE)
        tx1[s, :, 0:HD] = q2
        tx1[s, :, HD:384] = c.astype(BF16)
        tx1[s + 1, :, 0:HD] = q2
        tx1[s + 1, :, HD:384] = pltpu.roll(c, PAGE, axis=1).astype(BF16)
    rx1[me] = tx1[me]

    l_routes.wait()
    l_router.wait()
    named = [routes_v[i] == expert for i in range(3)]
    chosen = jnp.where(named[0] | named[1] | named[2], 1.0, 0.0)
    chosen = jnp.concatenate([chosen[0:1], chosen[1:2]], axis=1)
    row, lane = iota((128, 128), 0), iota((128, 128), 1)
    row_step = (row % 8) // 4
    natural = row_step * 64 + (row // 8) * 4 + row % 4
    chosen_at = jnp.sum(jnp.where(lane == natural, chosen, 0.0), axis=1, keepdims=True)
    before = (lane < natural) & (lane // 64 == row_step)
    rank = jnp.sum(jnp.where(before, chosen, 0.0), axis=1, keepdims=True).astype(jnp.int32)
    slot_at = rank + jnp.where(row_step == core, 0, CAP)
    picked = jnp.where((lane == slot_at) & (chosen_at > 0.5), 1.0, 0.0)
    spread[...] = picked.astype(BF16)
    pick[...] = jnp.transpose(picked)
    router_row = jnp.concatenate([router_v[...].astype(F32), jnp.zeros((1, 512 - W), F32)], axis=1)
    edge_row, edge_lane = iota((8, 512), 0), iota((8, 512), 1)
    edge[...] = jnp.where(
        edge_row == 0, router_row, jnp.where((edge_row == 1) & (edge_lane >= W) & (edge_lane < W + 2), 1.0, 0.0)
    ).astype(BF16)

    def padded(rows):
        return jnp.concatenate([rows, jnp.zeros((rows.shape[0], 512 - W), F32)], axis=1)

    l_resid.wait()
    l_gain.wait()
    owned = iota((8, 128), 0)
    owned = (owned // 4) * 64 + g_me * 4 + owned % 4 == iota((8, 128), 1)
    base_v[0:8] = padded(dot(jnp.where(owned, 1.0, 0.0).astype(BF16), resid_v[...].reshape(128, W)))
    base_v[8:16] = jnp.broadcast_to(padded(gain_v[...].astype(F32).reshape(1, W)), (8, 512))

    pl.semaphore_wait(barrier, len(ATTN_ORDER) + len(NEIGHBOURS))

    def spread_attn(phase, src_of, dst, slot):
        for step in ATTN_ORDER:
            peer = attn_peer(*step)
            remote(phase, src_of(peer), dst.at[slot], peer, slot, attn_id(peer)).start()

    def spread_group(phase, src_of, dst):
        for step in GROUP_ORDER:
            peer = group_peer(*step)
            remote(phase, src_of(peer), dst.at[g_me], peer, g_me, group_id(peer)).start()

    def await_all(phase, dst):
        every = dst.at[pl.ds(0, 15)]
        remote(phase, every, every, 0, 0, attn_id(me)).wait_recv()

    spread_attn(QUERY, lambda peer: tx1.at[peer], rx1, me)
    tell(0)

    l_pool.wait()
    l_mig.wait()
    l_t1.wait()
    l_pair.wait()
    t8 = jnp.concatenate([tab1[...], t2], axis=0)
    q32 = jnp.concatenate([q8[:, h * HD:(h + 1) * HD] for h in range(4)], axis=0)
    q32b = q32.astype(BF16)
    pair8 = jnp.concatenate([pair_v[0].astype(F32), pair_v[1].astype(F32)], axis=0)
    peak = jnp.full((32, 128), NONE, F32)
    all_counts = []
    for c in range(TOKENS // CHUNK):
        pages = CHUNK // PAGE
        count = counts(t8, len8, c * pages, CHUNK)
        count = jnp.concatenate([count] * 4, axis=0)
        s = dot_nt(q32b, pool[c * pages:(c + 1) * pages, :, 0:HD].reshape(CHUNK, HD)) * SCALE
        s = jnp.where(count > 0.5, s, NONE)
        score[0, :, c * CHUNK:(c + 1) * CHUNK] = s
        score[1, :, c * CHUNK:(c + 1) * CHUNK] = count
        for b in range(CHUNK // 128):
            peak = jnp.maximum(peak, s[:, b * 128:(b + 1) * 128])
    m_local = jnp.max(peak, axis=1, keepdims=True)
    sums = jnp.zeros((32, 128), F32)
    o_local = jnp.zeros((32, HD), F32)
    for c in range(TOKENS // CHUNK):
        count = score[1, :, c * CHUNK:(c + 1) * CHUNK]
        weight = jnp.where(count > 0.5, count * jnp.exp(score[0, :, c * CHUNK:(c + 1) * CHUNK] - m_local), 0.0)
        for b in range(CHUNK // 128):
            sums = sums + weight[:, b * 128:(b + 1) * 128]
        pages = CHUNK // PAGE
        o_local = o_local + dot(
            weight.astype(BF16), pool[c * pages:(c + 1) * pages, :, HD:2 * HD].reshape(CHUNK, HD)
        )
    l_local = jnp.sum(sums, axis=1, keepdims=True)
    key32 = jnp.concatenate([pair8[:, 0:HD]] * 4, axis=0)
    value32 = jnp.concatenate([pair8[:, HD:2 * HD]] * 4, axis=0)
    own_score = jnp.sum(q32 * key32, axis=1, keepdims=True) * SCALE

    for dx in NEAR_FIRST:
        if dx == 1:
            hear(0)
            tell(1)
        steps = [(dx, dy, dc) for dy in (0, 1) for dc in (0, 1)]
        sources = [attn_peer(*step) for step in steps]
        for step, source in zip(steps, sources):
            if step != (0, 0, 0):
                remote(QUERY, tx1.at[source], rx1.at[source], source, source, attn_id(me)).wait_recv()
        pages = [migrations[0, source] for source in sources]
        asked = [rx1[source] for source in sources]
        count = jnp.concatenate([a[:, HD:HD + PAGE].astype(F32) for a in asked], axis=0)
        s = jnp.concatenate([dot_nt(a[:, 0:HD], pool[page, :, 0:HD]) for a, page in zip(asked, pages)], axis=0) * SCALE
        live = count > 0.5
        top = jnp.max(jnp.where(live, s, NONE), axis=1, keepdims=True).astype(BF16).astype(F32)
        weight = jnp.where(live, count * jnp.exp(s - top), 0.0)
        total = jnp.sum(weight, axis=1, keepdims=True)
        high = total.astype(BF16).astype(F32)
        at = iota((64, 128), 1)
        stat = jnp.where(at == 0, top, jnp.where(at == 1, high, jnp.where(at == 2, total - high, 0.0))).astype(BF16)
        weight = weight.astype(BF16)
        for i, (step, source) in enumerate(zip(steps, sources)):
            tx2[source, :, 0:HD] = dot(weight[16 * i:16 * i + 16], pool[pages[i], :, HD:2 * HD]).astype(BF16)
            tx2[source, :, HD:384] = stat[16 * i:16 * i + 16]
        for step, source in zip(steps, sources):
            if step != (0, 0, 0):
                remote(PARTIAL, tx2.at[source], rx2.at[me], source, me, attn_id(source)).start()
    rx2[me] = tx2[me]
    hear(1)
    tell(2)

    def of_step(rows, i):
        return jnp.concatenate([rows[8 * h + 4 * i:8 * h + 4 * i + 4] for h in range(4)], axis=0)

    top = jnp.maximum(m_local, own_score)
    f_local, f_own = jnp.exp(m_local - top), jnp.exp(own_score - top)
    above = f_local * o_local + f_own.astype(BF16).astype(F32) * value32
    first_step = of_step(above / (f_local * l_local + f_own), 0).astype(BF16)
    tx3[0] = first_step
    rx3[0, me] = first_step
    spread_attn(HEADS_FIRST, lambda peer: tx3.at[0], rx3.at[0], me)

    await_all(PARTIAL, rx2)
    back = rx2[...].astype(F32)
    m_s = back[:, :, HD:HD + 1]
    l_s = back[:, :, HD + 1:HD + 2] + back[:, :, HD + 2:HD + 3]
    m_r = jnp.max(m_s, axis=0)
    w_s = jnp.exp(m_s - m_r[None])
    l_r = jnp.sum(w_s * l_s, axis=0)
    o_r = jnp.sum(w_s * back[:, :, 0:HD], axis=0)
    m_near, l_near, o_near = of_step(m_local, 1), of_step(l_local, 1), of_step(o_local, 1)
    own_near = of_step(own_score, 1)
    top = jnp.maximum(jnp.maximum(m_near, m_r), own_near)
    f_near, f_far, f_own = jnp.exp(m_near - top), jnp.exp(m_r - top), jnp.exp(own_near - top)
    below = f_near * l_near + f_far * l_r + f_own
    above = f_near * o_near + f_far * o_r + f_own.astype(BF16).astype(F32) * of_step(value32, 1)
    second_step = (above / below).astype(BF16)
    tx3[1] = second_step
    rx3[1, me] = second_step
    spread_attn(HEADS_OUT, lambda peer: tx3.at[1], rx3.at[1], me)
    hear(2)
    tell(3)
    l_wo.wait()
    await_all(HEADS_FIRST, rx3.at[0])
    await_all(HEADS_OUT, rx3.at[1])

    steps = [rx3[i].astype(F32).reshape(NA, 2, 8, HD) for i in range(2)]
    turned = [jnp.concatenate([t[:, :, 4:8], t[:, :, 0:4]], axis=2) for t in steps]
    upper = iota((NA, 2, 8, HD), 2) < 4
    x = [
        jnp.where(upper, steps[0], turned[1]).astype(BF16),
        jnp.where(upper, turned[0], steps[1]).astype(BF16),
    ]
    partial = jnp.zeros((128, W), F32)
    for h in range(4):
        partial = partial + dot_nt(x[h % 2][:, h // 2].reshape(128, HD), wo[:, h * HD:(h + 1) * HD])

    tx4[...] = fold(padded(partial).reshape(NG, 8, 512)).astype(BF16)
    rx4[g_me] = tx4[g_me]
    hear(3)
    spread_group(PROJ, lambda peer: tx4.at[peer], rx4)

    await_all(PROJ, rx4)
    hidden = base_v[0:8] + unfold(jnp.sum(rx4[...].astype(F32), axis=0))
    hidden_v[...] = hidden
    squares = jnp.sum(hidden * hidden, axis=1, keepdims=True)
    high = squares.astype(BF16).astype(F32)
    scaled = hidden * base_v[8:16]
    scaled = jnp.where(edge_lane == W, high, jnp.where(edge_lane == W + 1, squares - high, scaled))
    scaled = fold(scaled).astype(BF16)
    tx5[...] = scaled
    rx5[g_me] = scaled
    spread_group(ROWS_IN, lambda peer: tx5, rx5)
    await_all(ROWS_IN, rx5)

    rows = unfold(rx5[...].astype(F32)).reshape(128, 512).astype(BF16)
    rows_v[...] = rows
    stats = dot_nt(edge[...], rows)
    tx6[...] = stats
    rx6[me] = stats
    spread_attn(STATS, lambda peer: tx6, rx6, me)
    slots_v[...] = dot(pick[0:2 * CAP, :].astype(BF16), rows_v[:, 0:W]).astype(BF16)

    l_wg.wait()
    l_wu.wait()
    left = iota((2 * CAP, 128), 1) < 64

    def compute_pair(p):
        lanes = pl.ds(pl.multiple_of(640 * p, 128), 640)
        g = dot(slots_v[...], wg[:, lanes])
        u = dot(slots_v[...], wu[:, lanes])
        g2, u2 = g[:, 256:384], pltpu.roll(u[:, 256:384], 64, axis=1)
        pieces = (
            (g[:, 0:256], u[:, 0:256], jnp.where(left, g2, u2)),
            (g[:, 384:640], u[:, 384:640], jnp.where(left, u2, g2)),
        )
        for i in range(2):
            piece = jnp.concatenate(pieces[i], axis=1)
            j = 2 * p + i
            own_v[j] = piece[0:CAP]
            txs[j] = piece[CAP:2 * CAP].astype(BF16)
            remote(SIBLING, txs.at[j], rxs.at[j], j, j, attn_id(sibling)).start()

    def reduce_pair(dx):
        for dy in (1, 0):
            j = chip_peer(dx, dy)
            remote(SIBLING, txs.at[j], rxs.at[j], j, j, attn_id(sibling)).wait_recv()
            tx7[j] = (own_v[j] + rxs[j].astype(F32)).astype(BF16)
            if (dx, dy) != (0, 0):
                remote(REDUCE, tx7.at[j], rx7.at[chip], j, chip, attn_id(2 * j + core)).start()

    far_first = (2, 1, 3, 0)
    for k, dx in enumerate(far_first):
        compute_pair(lax.rem(at_x + dx, 4))
        if k > 0:
            reduce_pair(far_first[k - 1])
    reduce_pair(0)

    await_all(STATS, rx6)
    stats = jnp.sum(rx6[...], axis=0)
    inverse_row = lax.rsqrt(stats[1:2] / D + EPSILON)
    route_row = 1.0 / (1.0 + jnp.exp(-(stats[0:1] * inverse_row)))
    picked = pick[0:2 * CAP, :]
    inverse = jnp.sum(picked[0:CAP] * inverse_row, axis=1, keepdims=True)
    route = jnp.sum(picked * route_row, axis=1, keepdims=True)

    total = tx7[chip].astype(F32)
    for dx in NEAR_FIRST:
        for dy in (0, 1):
            if (dx, dy) != (0, 0):
                j = chip_peer(dx, dy)
                remote(REDUCE, tx7.at[j], rx7.at[j], j, j, attn_id(me)).wait_recv()
                total = total + rx7[j].astype(F32)
    total = total * inverse
    mixed = total[:, 512:640]
    half = silu(mixed) * pltpu.roll(mixed, 64, axis=1)
    right = jnp.where(iota((CAP, 128), 1) < 64, 0, 1)
    half = jnp.where(right == lax.rem(chip, 2), half, 0.0)
    activated = jnp.concatenate([silu(total[:, 0:256]) * total[:, 256:512], half], axis=1).astype(BF16)
    tx8[...] = activated
    rx8[0, chip] = activated
    for dx in far_first:
        for dy in (1, 0):
            if (dx, dy) != (0, 0):
                j = chip_peer(dx, dy)
                remote(ACT, tx8, rx8.at[0, chip], j, chip, attn_id(2 * j + core)).start()
    remote(FORWARD, tx8, rx8.at[1, chip], chip, chip, attn_id(sibling)).start()
    l_wd.wait()

    def forward_pair(dx):
        for dy in (0, 1):
            if (dx, dy) != (0, 0):
                j = chip_peer(dx, dy)
                remote(ACT, tx8, rx8.at[0, j], j, j, attn_id(me)).wait_recv()
                remote(FORWARD, rx8.at[0, j], rx8.at[1, j], j, j, attn_id(sibling)).start()

    def down_pair(dx):
        p = lax.rem(at_x + dx, 4)
        for j in (2 * p, 2 * p + 1):
            remote(FORWARD, tx8, rx8.at[1, j], j, j, attn_id(me)).wait_recv()
        parts = []
        for side in range(2):
            a, b = rx8[side, 2 * p], rx8[side, 2 * p + 1]
            middle = (a[:, 256:384].astype(F32) + b[:, 256:384].astype(F32)).astype(BF16)
            parts.append(jnp.concatenate([a[:, 0:256], middle, b[:, 0:256]], axis=1))
        lanes = pl.ds(pl.multiple_of(640 * p, 128), 640)
        return dot_nt(jnp.concatenate(parts, axis=0), wd[:, lanes])

    result = jnp.zeros((2 * CAP, W), F32)
    for k, dx in enumerate(NEAR_FIRST):
        forward_pair(dx)
        if k > 0:
            result = result + down_pair(NEAR_FIRST[k - 1])
    result = result + down_pair(NEAR_FIRST[3])
    result = (result * route).astype(BF16)
    added = dot(spread[:, 0:2 * CAP], result)
    tx9[...] = fold(padded(added).reshape(NG, 8, 512)).astype(BF16)
    rx9[g_me] = tx9[g_me]
    spread_group(BACK, lambda peer: tx9.at[peer], rx9)

    def sent(phase, every):
        remote(phase, every, every, 0, 0, attn_id(me)).wait_send()

    for phase, dst in ((QUERY, rx1), (PARTIAL, rx2), (HEADS_FIRST, rx3.at[0]), (HEADS_OUT, rx3.at[1]), (PROJ, rx4), (ROWS_IN, rx5), (STATS, rx6), (BACK, rx9)):
        sent(phase, dst.at[pl.ds(0, 15)])
    sent(SIBLING, txs)
    sent(REDUCE, tx7.at[pl.ds(0, CHIPS - 1)])
    sent(ACT, rx8.at[0, pl.ds(0, CHIPS - 1)])
    sent(FORWARD, rx8.at[0])
    await_all(BACK, rx9)
    final = hidden_v[...] + unfold(jnp.sum(rx9[...].astype(F32), axis=0))
    out[0] = final[0:4, 0:W].astype(BF16)
    out[1] = final[4:8, 0:W].astype(BF16)


def on_device(
    queries, new_pairs, kv_pool, table_first, table_second, lengths, migrations, residual,
    out_proj, norm_gain, router, routes, gate_weight, up_weight, down_weight,
):
    vmem, smem = pltpu.VMEM, pltpu.SMEM
    return pl.pallas_call(
        body,
        out_shape=jax.ShapeDtypeStruct((2, 4, W), BF16),
        in_specs=[pl.BlockSpec(memory_space=pltpu.HBM)] * 15,
        out_specs=pl.BlockSpec(memory_space=pltpu.VMEM),
        scratch_shapes=[
            smem((2, 4), jnp.int32), smem((1, 16), jnp.int32),
            vmem((2, 4, 1024), BF16), vmem((2, 4, 512), BF16), vmem((LOCAL, PAGE, 2 * HD), BF16),
            vmem((4, 16), jnp.int32), vmem((4, 16), jnp.int32), vmem((2, 64, W), BF16), vmem((W, 1024), BF16),
            vmem((W,), BF16), vmem((1, W), BF16), vmem((3, 2, 64), jnp.int32),
            vmem((W, 2560), BF16), vmem((W, 2560), BF16), vmem((W, 2560), BF16),
            pltpu.SemaphoreType.DMA((15,)), pltpu.SemaphoreType.DMA((12,)), pltpu.SemaphoreType.DMA((12, 16)), pltpu.SemaphoreType.REGULAR((4,)),
            vmem((NA, 16, 384), BF16), vmem((NA, 16, 384), BF16),
            vmem((NA, 16, 384), BF16), vmem((NA, 16, 384), BF16),
            vmem((2, 16, HD), BF16), vmem((2, NA, 16, HD), BF16),
            vmem((NG, 16, 256), BF16), vmem((NG, 16, 256), BF16),
            vmem((16, 256), BF16), vmem((NG, 16, 256), BF16),
            vmem((8, 128), F32), vmem((NA, 8, 128), F32),
            vmem((CHIPS, CAP, 640), BF16), vmem((CHIPS, CAP, 640), BF16),
            vmem((CHIPS, CAP, 640), BF16), vmem((CHIPS, CAP, 640), BF16),
            vmem((CAP, 384), BF16), vmem((2, CHIPS, CAP, 384), BF16),
            vmem((NG, 16, 256), BF16), vmem((NG, 16, 256), BF16),
            vmem((2, 32, TOKENS), F32), vmem((16, 512), F32), vmem((8, 512), F32), vmem((2 * CAP, W), BF16), vmem((128, 512), BF16),
            vmem((128, 128), F32), vmem((128, 128), BF16), vmem((8, 512), BF16), vmem((CHIPS, CAP, 640), F32),
        ],
        compiler_params=pltpu.CompilerParams(
            collective_id=0, has_side_effects=True, vmem_limit_bytes=60 * 1024 * 1024
        ),
        name="layer",
    )(
        queries, new_pairs, kv_pool, table_first, table_second, lengths, migrations, residual,
        out_proj.T, norm_gain, router.T, routes.transpose(2, 0, 1), gate_weight, up_weight, down_weight[0].T,
    )


def solution(mesh):
    return jax.shard_map(
        on_device,
        mesh=mesh,
        in_specs=(
            P(None, "attn", ("ffn", "tp")),
            P(None, "attn", None),
            P("attn", None, None),
            P("attn", None),
            P("attn", None),
            P(None, "attn"),
            P("attn", None),
            P(None, None, "attn"),
            P(("ffn", "tp"), "attn"),
            P("attn"),
            P("attn", "ffn"),
            P(),
            P("ffn", "attn", "tp"),
            P("ffn", "attn", "tp"),
            P("ffn", "tp", "attn"),
        ),
        out_specs=P(None, ("ffn", "tp"), "attn"),
        check_vma=False,
    )
```

```python
import jax
import jax.numpy as jnp
from jax import lax
from jax.experimental import pallas as pl
from jax.experimental.pallas import tpu as pltpu
from jax.sharding import PartitionSpec as P

F32, BF16 = jnp.float32, jnp.bfloat16
MESH = pl.DeviceIdType.MESH
D = 7168
EPSILON = 1e-6
NA, NG = 16, 16
CHIPS = 8
LOCAL = 48
PAGE, HD = 64, 256
TOKENS = LOCAL * PAGE
CHUNK = 512
CAP = 48
W = 448
NONE = -1e30
SCALE = HD ** -0.5
NT_DIMS = (((1,), (1,)), ((), ()))
ATTN_ORDER = [(dx, dy, dc) for dx in (2, 1, 3, 0) for dy in (1, 0) for dc in (0, 1) if (dx, dy, dc) != (0, 0, 0)]
GROUP_ORDER = [(dz, dt) for dt in (1, 0) for dz in (4, 3, 5, 2, 6, 1, 7, 0) if (dz, dt) != (0, 0)]
NEIGHBOURS = [(0, 1), (1, 0), (7, 0)]
NEAR_FIRST = (0, 1, 3, 2)
QUERY, PARTIAL, HEADS_OUT, PROJ, ROWS_IN, STATS, SIBLING, REDUCE, ACT, FORWARD, BACK, HEADS_FIRST = range(12)
TOGETHER = (PARTIAL, HEADS_OUT, PROJ, ROWS_IN, STATS, BACK, HEADS_FIRST)


def iota(shape, axis):
    return lax.broadcasted_iota(jnp.int32, shape, axis)


def dot(a, b):
    return jnp.dot(a, b, preferred_element_type=F32)


def dot_nt(a, b):
    return lax.dot_general(a, b, NT_DIMS, preferred_element_type=F32)


def fold(block):
    return jnp.concatenate([block[..., :256], block[..., 256:]], axis=-2)


def unfold(block):
    return jnp.concatenate([block[..., :8, :], block[..., 8:, :]], axis=-1)


def silu(v):
    return v / (1.0 + jnp.exp(-v))


def body(
    queries, new_pairs, kv_pool, table_first, table_second, lengths_in, migrations_in, residual,
    out_proj, norm_gain, router, routes, gate_weight, up_weight, down_weight,
    out,
    lengths, migrations, q_v, pair_v, pool, tab1, tab2, resid_v, wo, gain_v, router_v, routes_v, wg, wu, wd,
    load_sem, send, recv, gossip,
    tx1, rx1, tx2, rx2, tx3, rx3, tx4, rx4, tx5, rx5, tx6, rx6, txs, rxs, tx7, rx7, tx8, rx8, tx9, rx9,
    score, base_v, hidden_v, slots_v, rows_v, pick, spread, edge, own_v,
):
    me = lax.axis_index("attn")
    expert = lax.axis_index("ffn")
    g_me = expert * 2 + lax.axis_index("tp")
    core = lax.rem(me, 2)
    chip = me // 2
    sibling = me + 1 - 2 * core
    at_x, at_y = me // 4, lax.rem(chip, 2)
    at_t = lax.rem(g_me, 2)

    def attn_peer(dx, dy, dc):
        return lax.rem(at_x + dx, 4) * 4 + lax.rem(at_y + dy, 2) * 2 + lax.rem(core + dc, 2)

    def chip_peer(dx, dy):
        return lax.rem(at_x + dx, 4) * 2 + lax.rem(at_y + dy, 2)

    def group_peer(dz, dt):
        return lax.rem(expert + dz, 8) * 2 + lax.rem(at_t + dt, 2)

    pairs = [
        (queries, q_v), (table_second, tab2), (table_first, tab1), (new_pairs, pair_v),
        (lengths_in, lengths), (migrations_in, migrations),
        (kv_pool.at[pl.ds(0, LOCAL)], pool), (routes, routes_v), (router, router_v), (norm_gain, gain_v),
        (residual, resid_v), (out_proj, wo), (gate_weight.at[0], wg), (up_weight.at[0], wu), (down_weight, wd),
    ]
    loads = [pltpu.make_async_copy(src, dst, load_sem.at[i]) for i, (src, dst) in enumerate(pairs)]
    for load in loads:
        load.start()
    (l_q, l_t2, l_t1, l_pair, l_len, l_mig, l_pool, l_routes, l_router, l_gain, l_resid, l_wo, l_wg, l_wu, l_wd) = loads

    def attn_id(i):
        return {"attn": i}

    def group_id(g):
        return {"ffn": g // 2, "tp": lax.rem(g, 2)}

    barrier = pltpu.get_barrier_semaphore()

    for step in ATTN_ORDER:
        pl.semaphore_signal(barrier, inc=1, device_id=attn_id(attn_peer(*step)), device_id_type=MESH)
    for step in NEIGHBOURS:
        pl.semaphore_signal(barrier, inc=1, device_id=group_id(group_peer(*step)), device_id_type=MESH)

    def tell(i):
        for dz in (1, 7):
            pl.semaphore_signal(gossip.at[i], inc=1, device_id=group_id(group_peer(dz, 0)), device_id_type=MESH)

    def hear(i):
        pl.semaphore_wait(gossip.at[i], 2)

    def remote(phase, src, dst, slot_to, slot_from, device):
        return pltpu.make_async_remote_copy(
            src_ref=src, dst_ref=dst, send_sem=send.at[phase], recv_sem=recv.at[phase, 0 if phase in TOGETHER else slot_from],
            device_id=device, device_id_type=MESH,
        )

    l_q.wait()
    l_t2.wait()
    l_len.wait()
    q8 = jnp.concatenate([q_v[0].astype(F32), q_v[1].astype(F32)], axis=0)
    t2 = tab2[...]
    t2x = jnp.concatenate([t2, t2, t2, t2], axis=0)

    def column(rows, values):
        at = iota((rows, 1), 0)
        result = jnp.zeros((rows, 1), jnp.int32)
        for i in range(rows):
            result = jnp.where(at == i, values[i], result)
        return result

    len2 = column(16, [lengths[1, i % 4] for i in range(16)])
    len8 = column(8, [lengths[i // 4, i % 4] for i in range(8)])

    def counts(table, length, first, width):
        lane = iota((table.shape[0], width), 1)
        page, place = first + lane // PAGE, lane % PAGE
        total = jnp.zeros((table.shape[0], width), F32)
        for k in range(16):
            left = length - k * PAGE
            total = total + jnp.where((page == table[:, k:k + 1]) & (place < left), 1.0, 0.0)
        return total

    q2 = jnp.concatenate([q8[4:8, h * HD:(h + 1) * HD] for h in range(4)], axis=0).astype(BF16)
    for s in range(0, NA, 2):
        c = counts(t2x, len2, LOCAL + s, 2 * PAGE)
        tx1[s, :, 0:HD] = q2
        tx1[s, :, HD:384] = c.astype(BF16)
        tx1[s + 1, :, 0:HD] = q2
        tx1[s + 1, :, HD:384] = pltpu.roll(c, PAGE, axis=1).astype(BF16)
    rx1[me] = tx1[me]

    l_routes.wait()
    l_router.wait()
    named = [routes_v[i] == expert for i in range(3)]
    chosen = jnp.where(named[0] | named[1] | named[2], 1.0, 0.0)
    chosen = jnp.concatenate([chosen[0:1], chosen[1:2]], axis=1)
    row, lane = iota((128, 128), 0), iota((128, 128), 1)
    row_step = (row % 8) // 4
    natural = row_step * 64 + (row // 8) * 4 + row % 4
    chosen_at = jnp.sum(jnp.where(lane == natural, chosen, 0.0), axis=1, keepdims=True)
    before = (lane < natural) & (lane // 64 == row_step)
    rank = jnp.sum(jnp.where(before, chosen, 0.0), axis=1, keepdims=True).astype(jnp.int32)
    slot_at = rank + jnp.where(row_step == core, 0, CAP)
    picked = jnp.where((lane == slot_at) & (chosen_at > 0.5), 1.0, 0.0)
    spread[...] = picked.astype(BF16)
    pick[...] = jnp.transpose(picked)
    router_row = jnp.concatenate([router_v[...].astype(F32), jnp.zeros((1, 512 - W), F32)], axis=1)
    edge_row, edge_lane = iota((8, 512), 0), iota((8, 512), 1)
    edge[...] = jnp.where(
        edge_row == 0, router_row, jnp.where((edge_row == 1) & (edge_lane >= W) & (edge_lane < W + 2), 1.0, 0.0)
    ).astype(BF16)

    def padded(rows):
        return jnp.concatenate([rows, jnp.zeros((rows.shape[0], 512 - W), F32)], axis=1)

    l_resid.wait()
    l_gain.wait()
    owned = iota((8, 128), 0)
    owned = (owned // 4) * 64 + g_me * 4 + owned % 4 == iota((8, 128), 1)
    base_v[0:8] = padded(dot(jnp.where(owned, 1.0, 0.0).astype(BF16), resid_v[...].reshape(128, W)))
    base_v[8:16] = jnp.broadcast_to(padded(gain_v[...].astype(F32).reshape(1, W)), (8, 512))

    pl.semaphore_wait(barrier, len(ATTN_ORDER) + len(NEIGHBOURS))

    def spread_attn(phase, src_of, dst, slot):
        for step in ATTN_ORDER:
            peer = attn_peer(*step)
            remote(phase, src_of(peer), dst.at[slot], peer, slot, attn_id(peer)).start()

    def spread_group(phase, src_of, dst):
        for step in GROUP_ORDER:
            peer = group_peer(*step)
            remote(phase, src_of(peer), dst.at[g_me], peer, g_me, group_id(peer)).start()

    def await_all(phase, dst):
        every = dst.at[pl.ds(0, 15)]
        remote(phase, every, every, 0, 0, attn_id(me)).wait_recv()

    spread_attn(QUERY, lambda peer: tx1.at[peer], rx1, me)
    tell(0)

    l_pool.wait()
    l_mig.wait()
    l_t1.wait()
    l_pair.wait()
    t8 = jnp.concatenate([tab1[...], t2], axis=0)
    q32 = jnp.concatenate([q8[:, h * HD:(h + 1) * HD] for h in range(4)], axis=0)
    q32b = q32.astype(BF16)
    pair8 = jnp.concatenate([pair_v[0].astype(F32), pair_v[1].astype(F32)], axis=0)
    peak = jnp.full((32, 128), NONE, F32)
    all_counts = []
    for c in range(TOKENS // CHUNK):
        pages = CHUNK // PAGE
        count = counts(t8, len8, c * pages, CHUNK)
        count = jnp.concatenate([count] * 4, axis=0)
        s = dot_nt(q32b, pool[c * pages:(c + 1) * pages, :, 0:HD].reshape(CHUNK, HD)) * SCALE
        s = jnp.where(count > 0.5, s, NONE)
        score[0, :, c * CHUNK:(c + 1) * CHUNK] = s
        score[1, :, c * CHUNK:(c + 1) * CHUNK] = count
        for b in range(CHUNK // 128):
            peak = jnp.maximum(peak, s[:, b * 128:(b + 1) * 128])
    m_local = jnp.max(peak, axis=1, keepdims=True)
    sums = jnp.zeros((32, 128), F32)
    o_local = jnp.zeros((32, HD), F32)
    for c in range(TOKENS // CHUNK):
        count = score[1, :, c * CHUNK:(c + 1) * CHUNK]
        weight = jnp.where(count > 0.5, count * jnp.exp(score[0, :, c * CHUNK:(c + 1) * CHUNK] - m_local), 0.0)
        for b in range(CHUNK // 128):
            sums = sums + weight[:, b * 128:(b + 1) * 128]
        pages = CHUNK // PAGE
        o_local = o_local + dot(
            weight.astype(BF16), pool[c * pages:(c + 1) * pages, :, HD:2 * HD].reshape(CHUNK, HD)
        )
    l_local = jnp.sum(sums, axis=1, keepdims=True)
    key32 = jnp.concatenate([pair8[:, 0:HD]] * 4, axis=0)
    value32 = jnp.concatenate([pair8[:, HD:2 * HD]] * 4, axis=0)
    own_score = jnp.sum(q32 * key32, axis=1, keepdims=True) * SCALE

    for dx in (2, 1, 3, 0):
        if dx == 1:
            hear(0)
            tell(1)
        steps = [(dx, dy, dc) for dy in (0, 1) for dc in (0, 1)]
        sources = [attn_peer(*step) for step in steps]
        for step, source in zip(steps, sources):
            if step != (0, 0, 0):
                remote(QUERY, tx1.at[source], rx1.at[source], source, source, attn_id(me)).wait_recv()
        pages = [migrations[0, source] for source in sources]
        asked = [rx1[source] for source in sources]
        count = jnp.concatenate([a[:, HD:HD + PAGE].astype(F32) for a in asked], axis=0)
        s = jnp.concatenate([dot_nt(a[:, 0:HD], pool[page, :, 0:HD]) for a, page in zip(asked, pages)], axis=0) * SCALE
        live = count > 0.5
        top = jnp.max(jnp.where(live, s, NONE), axis=1, keepdims=True).astype(BF16).astype(F32)
        weight = jnp.where(live, count * jnp.exp(s - top), 0.0)
        total = jnp.sum(weight, axis=1, keepdims=True)
        high = total.astype(BF16).astype(F32)
        at = iota((64, 128), 1)
        stat = jnp.where(at == 0, top, jnp.where(at == 1, high, jnp.where(at == 2, total - high, 0.0))).astype(BF16)
        weight = weight.astype(BF16)
        for i, (step, source) in enumerate(zip(steps, sources)):
            tx2[source, :, 0:HD] = dot(weight[16 * i:16 * i + 16], pool[pages[i], :, HD:2 * HD]).astype(BF16)
            tx2[source, :, HD:384] = stat[16 * i:16 * i + 16]
        for step, source in zip(steps, sources):
            if step != (0, 0, 0):
                remote(PARTIAL, tx2.at[source], rx2.at[me], source, me, attn_id(source)).start()
    rx2[me] = tx2[me]
    hear(1)
    tell(2)

    def of_step(rows, i):
        return jnp.concatenate([rows[8 * h + 4 * i:8 * h + 4 * i + 4] for h in range(4)], axis=0)

    top = jnp.maximum(m_local, own_score)
    f_local, f_own = jnp.exp(m_local - top), jnp.exp(own_score - top)
    above = f_local * o_local + f_own.astype(BF16).astype(F32) * value32
    first_step = of_step(above / (f_local * l_local + f_own), 0).astype(BF16)
    tx3[0] = first_step
    rx3[0, me] = first_step
    spread_attn(HEADS_FIRST, lambda peer: tx3.at[0], rx3.at[0], me)

    await_all(PARTIAL, rx2)
    back = rx2[...].astype(F32)
    m_s = back[:, :, HD:HD + 1]
    l_s = back[:, :, HD + 1:HD + 2] + back[:, :, HD + 2:HD + 3]
    m_r = jnp.max(m_s, axis=0)
    w_s = jnp.exp(m_s - m_r[None])
    l_r = jnp.sum(w_s * l_s, axis=0)
    o_r = jnp.sum(w_s * back[:, :, 0:HD], axis=0)
    m_near, l_near, o_near = of_step(m_local, 1), of_step(l_local, 1), of_step(o_local, 1)
    own_near = of_step(own_score, 1)
    top = jnp.maximum(jnp.maximum(m_near, m_r), own_near)
    f_near, f_far, f_own = jnp.exp(m_near - top), jnp.exp(m_r - top), jnp.exp(own_near - top)
    below = f_near * l_near + f_far * l_r + f_own
    above = f_near * o_near + f_far * o_r + f_own.astype(BF16).astype(F32) * of_step(value32, 1)
    second_step = (above / below).astype(BF16)
    tx3[1] = second_step
    rx3[1, me] = second_step
    spread_attn(HEADS_OUT, lambda peer: tx3.at[1], rx3.at[1], me)
    hear(2)
    tell(3)
    l_wo.wait()
    await_all(HEADS_FIRST, rx3.at[0])
    await_all(HEADS_OUT, rx3.at[1])

    steps = [rx3[i].astype(F32).reshape(NA, 2, 8, HD) for i in range(2)]
    turned = [jnp.concatenate([t[:, :, 4:8], t[:, :, 0:4]], axis=2) for t in steps]
    upper = iota((NA, 2, 8, HD), 2) < 4
    x = [
        jnp.where(upper, steps[0], turned[1]).astype(BF16),
        jnp.where(upper, turned[0], steps[1]).astype(BF16),
    ]
    partial = jnp.zeros((128, W), F32)
    for h in range(4):
        partial = partial + dot_nt(x[h % 2][:, h // 2].reshape(128, HD), wo[:, h * HD:(h + 1) * HD])

    tx4[...] = fold(padded(partial).reshape(NG, 8, 512)).astype(BF16)
    rx4[g_me] = tx4[g_me]
    hear(3)
    spread_group(PROJ, lambda peer: tx4.at[peer], rx4)

    await_all(PROJ, rx4)
    hidden = base_v[0:8] + unfold(jnp.sum(rx4[...].astype(F32), axis=0))
    hidden_v[...] = hidden
    squares = jnp.sum(hidden * hidden, axis=1, keepdims=True)
    high = squares.astype(BF16).astype(F32)
    scaled = hidden * base_v[8:16]
    scaled = jnp.where(edge_lane == W, high, jnp.where(edge_lane == W + 1, squares - high, scaled))
    scaled = fold(scaled).astype(BF16)
    tx5[...] = scaled
    rx5[g_me] = scaled
    spread_group(ROWS_IN, lambda peer: tx5, rx5)
    await_all(ROWS_IN, rx5)

    rows = unfold(rx5[...].astype(F32)).reshape(128, 512).astype(BF16)
    rows_v[...] = rows
    stats = dot_nt(edge[...], rows)
    tx6[...] = stats
    rx6[me] = stats
    spread_attn(STATS, lambda peer: tx6, rx6, me)
    slots_v[...] = dot(pick[0:2 * CAP, :].astype(BF16), rows_v[:, 0:W]).astype(BF16)

    l_wg.wait()
    l_wu.wait()
    left = iota((2 * CAP, 128), 1) < 64

    def compute_pair(p):
        lanes = pl.ds(pl.multiple_of(640 * p, 128), 640)
        g = dot(slots_v[...], wg[:, lanes])
        u = dot(slots_v[...], wu[:, lanes])
        g2, u2 = g[:, 256:384], pltpu.roll(u[:, 256:384], 64, axis=1)
        pieces = (
            (g[:, 0:256], u[:, 0:256], jnp.where(left, g2, u2)),
            (g[:, 384:640], u[:, 384:640], jnp.where(left, u2, g2)),
        )
        for i in range(2):
            piece = jnp.concatenate(pieces[i], axis=1)
            j = 2 * p + i
            own_v[j] = piece[0:CAP]
            txs[j] = piece[CAP:2 * CAP].astype(BF16)
            remote(SIBLING, txs.at[j], rxs.at[j], j, j, attn_id(sibling)).start()

    def reduce_pair(dx):
        for dy in (1, 0):
            j = chip_peer(dx, dy)
            remote(SIBLING, txs.at[j], rxs.at[j], j, j, attn_id(sibling)).wait_recv()
            tx7[j] = (own_v[j] + rxs[j].astype(F32)).astype(BF16)
            if (dx, dy) != (0, 0):
                remote(REDUCE, tx7.at[j], rx7.at[chip], j, chip, attn_id(2 * j + core)).start()

    far_first = (2, 1, 3, 0)
    for k, dx in enumerate(far_first):
        compute_pair(lax.rem(at_x + dx, 4))
        if k > 0:
            reduce_pair(far_first[k - 1])
    reduce_pair(0)

    await_all(STATS, rx6)
    stats = jnp.sum(rx6[...], axis=0)
    inverse_row = lax.rsqrt(stats[1:2] / D + EPSILON)
    route_row = 1.0 / (1.0 + jnp.exp(-(stats[0:1] * inverse_row)))
    picked = pick[0:2 * CAP, :]
    inverse = jnp.sum(picked[0:CAP] * inverse_row, axis=1, keepdims=True)
    route = jnp.sum(picked * route_row, axis=1, keepdims=True)

    total = tx7[chip].astype(F32)
    for dx in NEAR_FIRST:
        for dy in (0, 1):
            if (dx, dy) != (0, 0):
                j = chip_peer(dx, dy)
                remote(REDUCE, tx7.at[j], rx7.at[j], j, j, attn_id(me)).wait_recv()
                total = total + rx7[j].astype(F32)
    total = total * inverse
    mixed = total[:, 512:640]
    half = silu(mixed) * pltpu.roll(mixed, 64, axis=1)
    right = jnp.where(iota((CAP, 128), 1) < 64, 0, 1)
    half = jnp.where(right == lax.rem(chip, 2), half, 0.0)
    activated = jnp.concatenate([silu(total[:, 0:256]) * total[:, 256:512], half], axis=1).astype(BF16)
    tx8[...] = activated
    rx8[0, chip] = activated
    for dx in far_first:
        for dy in (1, 0):
            if (dx, dy) != (0, 0):
                j = chip_peer(dx, dy)
                remote(ACT, tx8, rx8.at[0, chip], j, chip, attn_id(2 * j + core)).start()
    remote(FORWARD, tx8, rx8.at[1, chip], chip, chip, attn_id(sibling)).start()
    l_wd.wait()

    def forward_pair(dx):
        for dy in (0, 1):
            if (dx, dy) != (0, 0):
                j = chip_peer(dx, dy)
                remote(ACT, tx8, rx8.at[0, j], j, j, attn_id(me)).wait_recv()
                remote(FORWARD, rx8.at[0, j], rx8.at[1, j], j, j, attn_id(sibling)).start()

    def down_pair(dx):
        p = lax.rem(at_x + dx, 4)
        for j in (2 * p, 2 * p + 1):
            remote(FORWARD, tx8, rx8.at[1, j], j, j, attn_id(me)).wait_recv()
        parts = []
        for side in range(2):
            a, b = rx8[side, 2 * p], rx8[side, 2 * p + 1]
            middle = (a[:, 256:384].astype(F32) + b[:, 256:384].astype(F32)).astype(BF16)
            parts.append(jnp.concatenate([a[:, 0:256], middle, b[:, 0:256]], axis=1))
        lanes = pl.ds(pl.multiple_of(640 * p, 128), 640)
        return dot_nt(jnp.concatenate(parts, axis=0), wd[:, lanes])

    result = jnp.zeros((2 * CAP, W), F32)
    for k, dx in enumerate(far_first):
        forward_pair(dx)
        if k > 0:
            result = result + down_pair(far_first[k - 1])
    result = result + down_pair(0)
    result = (result * route).astype(BF16)
    added = dot(spread[:, 0:2 * CAP], result)
    tx9[...] = fold(padded(added).reshape(NG, 8, 512)).astype(BF16)
    rx9[g_me] = tx9[g_me]
    spread_group(BACK, lambda peer: tx9.at[peer], rx9)

    def sent(phase, every):
        remote(phase, every, every, 0, 0, attn_id(me)).wait_send()

    for phase, dst in ((QUERY, rx1), (PARTIAL, rx2), (HEADS_FIRST, rx3.at[0]), (HEADS_OUT, rx3.at[1]), (PROJ, rx4), (ROWS_IN, rx5), (STATS, rx6), (BACK, rx9)):
        sent(phase, dst.at[pl.ds(0, 15)])
    sent(SIBLING, txs)
    sent(REDUCE, tx7.at[pl.ds(0, CHIPS - 1)])
    sent(ACT, rx8.at[0, pl.ds(0, CHIPS - 1)])
    sent(FORWARD, rx8.at[0])
    await_all(BACK, rx9)
    final = hidden_v[...] + unfold(jnp.sum(rx9[...].astype(F32), axis=0))
    out[0] = final[0:4, 0:W].astype(BF16)
    out[1] = final[4:8, 0:W].astype(BF16)


def on_device(
    queries, new_pairs, kv_pool, table_first, table_second, lengths, migrations, residual,
    out_proj, norm_gain, router, routes, gate_weight, up_weight, down_weight,
):
    vmem, smem = pltpu.VMEM, pltpu.SMEM
    return pl.pallas_call(
        body,
        out_shape=jax.ShapeDtypeStruct((2, 4, W), BF16),
        in_specs=[pl.BlockSpec(memory_space=pltpu.HBM)] * 15,
        out_specs=pl.BlockSpec(memory_space=pltpu.VMEM),
        scratch_shapes=[
            smem((2, 4), jnp.int32), smem((1, 16), jnp.int32),
            vmem((2, 4, 1024), BF16), vmem((2, 4, 512), BF16), vmem((LOCAL, PAGE, 2 * HD), BF16),
            vmem((4, 16), jnp.int32), vmem((4, 16), jnp.int32), vmem((2, 64, W), BF16), vmem((W, 1024), BF16),
            vmem((W,), BF16), vmem((1, W), BF16), vmem((3, 2, 64), jnp.int32),
            vmem((W, 2560), BF16), vmem((W, 2560), BF16), vmem((W, 2560), BF16),
            pltpu.SemaphoreType.DMA((15,)), pltpu.SemaphoreType.DMA((12,)), pltpu.SemaphoreType.DMA((12, 16)), pltpu.SemaphoreType.REGULAR((4,)),
            vmem((NA, 16, 384), BF16), vmem((NA, 16, 384), BF16),
            vmem((NA, 16, 384), BF16), vmem((NA, 16, 384), BF16),
            vmem((2, 16, HD), BF16), vmem((2, NA, 16, HD), BF16),
            vmem((NG, 16, 256), BF16), vmem((NG, 16, 256), BF16),
            vmem((16, 256), BF16), vmem((NG, 16, 256), BF16),
            vmem((8, 128), F32), vmem((NA, 8, 128), F32),
            vmem((CHIPS, CAP, 640), BF16), vmem((CHIPS, CAP, 640), BF16),
            vmem((CHIPS, CAP, 640), BF16), vmem((CHIPS, CAP, 640), BF16),
            vmem((CAP, 384), BF16), vmem((2, CHIPS, CAP, 384), BF16),
            vmem((NG, 16, 256), BF16), vmem((NG, 16, 256), BF16),
            vmem((2, 32, TOKENS), F32), vmem((16, 512), F32), vmem((8, 512), F32), vmem((2 * CAP, W), BF16), vmem((128, 512), BF16),
            vmem((128, 128), F32), vmem((128, 128), BF16), vmem((8, 512), BF16), vmem((CHIPS, CAP, 640), F32),
        ],
        compiler_params=pltpu.CompilerParams(
            collective_id=0, has_side_effects=True, vmem_limit_bytes=60 * 1024 * 1024
        ),
        name="layer",
    )(
        queries, new_pairs, kv_pool, table_first, table_second, lengths, migrations, residual,
        out_proj.T, norm_gain, router.T, routes.transpose(2, 0, 1), gate_weight, up_weight, down_weight[0].T,
    )


def solution(mesh):
    return jax.shard_map(
        on_device,
        mesh=mesh,
        in_specs=(
            P(None, "attn", ("ffn", "tp")),
            P(None, "attn", None),
            P("attn", None, None),
            P("attn", None),
            P("attn", None),
            P(None, "attn"),
            P("attn", None),
            P(None, None, "attn"),
            P(("ffn", "tp"), "attn"),
            P("attn"),
            P("attn", "ffn"),
            P(),
            P("ffn", "attn", "tp"),
            P("ffn", "attn", "tp"),
            P("ffn", "tp", "attn"),
        ),
        out_specs=P(None, ("ffn", "tp"), "attn"),
        check_vma=False,
    )
```

```python
import jax
import jax.numpy as jnp
from jax import lax
from jax.experimental import pallas as pl
from jax.experimental.pallas import tpu as pltpu
from jax.sharding import PartitionSpec as P

F32, BF16 = jnp.float32, jnp.bfloat16
MESH = pl.DeviceIdType.MESH
D = 7168
EPSILON = 1e-6
NA, NG = 16, 16
CHIPS = 8
LOCAL = 48
PAGE, HD = 64, 256
TOKENS = LOCAL * PAGE
CHUNK = 512
CAP = 48
W = 448
NONE = -1e30
SCALE = HD ** -0.5
NT_DIMS = (((1,), (1,)), ((), ()))
ATTN_ORDER = [(dx, dy, dc) for dx in (2, 1, 3, 0) for dy in (1, 0) for dc in (0, 1) if (dx, dy, dc) != (0, 0, 0)]
GROUP_ORDER = [(dz, dt) for dt in (1, 0) for dz in (4, 3, 5, 2, 6, 1, 7, 0) if (dz, dt) != (0, 0)]
NEIGHBOURS = [(0, 1), (1, 0), (7, 0)]
NEAR_FIRST = (0, 1, 3, 2)
CHIP_ORDER = [(dx, dy) for dx in (2, 1, 3, 0) for dy in (1, 0) if (dx, dy) != (0, 0)]
QUERY, PARTIAL, HEADS_OUT, PROJ, ROWS_IN, STATS, SIBLING, REDUCE, ACT, FORWARD, BACK, HEADS_FIRST, REDUCE_B, ACT_B, FORWARD_B = range(15)
TOGETHER = (PARTIAL, HEADS_OUT, PROJ, ROWS_IN, STATS, BACK, HEADS_FIRST)


def iota(shape, axis):
    return lax.broadcasted_iota(jnp.int32, shape, axis)


def dot(a, b):
    return jnp.dot(a, b, preferred_element_type=F32)


def dot_nt(a, b):
    return lax.dot_general(a, b, NT_DIMS, preferred_element_type=F32)


def fold(block):
    return jnp.concatenate([block[..., :256], block[..., 256:]], axis=-2)


def unfold(block):
    return jnp.concatenate([block[..., :8, :], block[..., 8:, :]], axis=-1)


def silu(v):
    return v / (1.0 + jnp.exp(-v))


def body(
    queries, new_pairs, kv_pool, table_first, table_second, lengths_in, migrations_in, residual,
    out_proj, norm_gain, router, routes, gate_weight, up_weight, down_weight,
    out,
    lengths, migrations, q_v, pair_v, pool, tab1, tab2, resid_v, wo, gain_v, router_v, routes_v, wg, wu, wd,
    load_sem, send, recv, gossip,
    tx1, rx1, tx2, rx2, tx3, rx3, tx4, rx4, tx5, rx5, tx6, rx6, txs, rxs, tx7, rx7, tx7b, rx7b, tx8, rx8, tx8b, rx8b, tx9, rx9,
    score, base_v, hidden_v, slots_v, rows_v, pick, spread, edge, own_v,
):
    me = lax.axis_index("attn")
    expert = lax.axis_index("ffn")
    g_me = expert * 2 + lax.axis_index("tp")
    core = lax.rem(me, 2)
    chip = me // 2
    sibling = me + 1 - 2 * core
    at_x, at_y = me // 4, lax.rem(chip, 2)
    at_t = lax.rem(g_me, 2)

    def attn_peer(dx, dy, dc):
        return lax.rem(at_x + dx, 4) * 4 + lax.rem(at_y + dy, 2) * 2 + lax.rem(core + dc, 2)

    def chip_peer(dx, dy):
        return lax.rem(at_x + dx, 4) * 2 + lax.rem(at_y + dy, 2)

    def group_peer(dz, dt):
        return lax.rem(expert + dz, 8) * 2 + lax.rem(at_t + dt, 2)

    pairs = [
        (queries, q_v), (table_second, tab2), (table_first, tab1), (new_pairs, pair_v),
        (lengths_in, lengths), (migrations_in, migrations),
        (kv_pool.at[pl.ds(0, LOCAL)], pool), (routes, routes_v), (router, router_v), (norm_gain, gain_v),
        (residual, resid_v), (out_proj, wo), (gate_weight.at[0], wg), (up_weight.at[0], wu), (down_weight, wd),
    ]
    loads = [pltpu.make_async_copy(src, dst, load_sem.at[i]) for i, (src, dst) in enumerate(pairs)]
    for load in loads:
        load.start()
    (l_q, l_t2, l_t1, l_pair, l_len, l_mig, l_pool, l_routes, l_router, l_gain, l_resid, l_wo, l_wg, l_wu, l_wd) = loads

    def attn_id(i):
        return {"attn": i}

    def group_id(g):
        return {"ffn": g // 2, "tp": lax.rem(g, 2)}

    barrier = pltpu.get_barrier_semaphore()

    for step in ATTN_ORDER:
        pl.semaphore_signal(barrier, inc=1, device_id=attn_id(attn_peer(*step)), device_id_type=MESH)
    for step in NEIGHBOURS:
        pl.semaphore_signal(barrier, inc=1, device_id=group_id(group_peer(*step)), device_id_type=MESH)

    def tell(i):
        for dz in (1, 7):
            pl.semaphore_signal(gossip.at[i], inc=1, device_id=group_id(group_peer(dz, 0)), device_id_type=MESH)

    def hear(i):
        pl.semaphore_wait(gossip.at[i], 2)

    def remote(phase, src, dst, slot_to, slot_from, device):
        return pltpu.make_async_remote_copy(
            src_ref=src, dst_ref=dst, send_sem=send.at[phase], recv_sem=recv.at[phase, 0 if phase in TOGETHER else slot_from],
            device_id=device, device_id_type=MESH,
        )

    l_q.wait()
    l_t2.wait()
    l_len.wait()
    q8 = jnp.concatenate([q_v[0].astype(F32), q_v[1].astype(F32)], axis=0)
    t2 = tab2[...]
    t2x = jnp.concatenate([t2, t2, t2, t2], axis=0)

    def column(rows, values):
        at = iota((rows, 1), 0)
        result = jnp.zeros((rows, 1), jnp.int32)
        for i in range(rows):
            result = jnp.where(at == i, values[i], result)
        return result

    len2 = column(16, [lengths[1, i % 4] for i in range(16)])
    len8 = column(8, [lengths[i // 4, i % 4] for i in range(8)])

    def counts(table, length, first, width):
        lane = iota((table.shape[0], width), 1)
        page, place = first + lane // PAGE, lane % PAGE
        total = jnp.zeros((table.shape[0], width), F32)
        for k in range(16):
            left = length - k * PAGE
            total = total + jnp.where((page == table[:, k:k + 1]) & (place < left), 1.0, 0.0)
        return total

    q2 = jnp.concatenate([q8[4:8, h * HD:(h + 1) * HD] for h in range(4)], axis=0).astype(BF16)
    for s in range(0, NA, 2):
        c = counts(t2x, len2, LOCAL + s, 2 * PAGE)
        tx1[s, :, 0:HD] = q2
        tx1[s, :, HD:384] = c.astype(BF16)
        tx1[s + 1, :, 0:HD] = q2
        tx1[s + 1, :, HD:384] = pltpu.roll(c, PAGE, axis=1).astype(BF16)
    rx1[me] = tx1[me]

    l_routes.wait()
    l_router.wait()
    named = [routes_v[i] == expert for i in range(3)]
    chosen = jnp.where(named[0] | named[1] | named[2], 1.0, 0.0)
    chosen = jnp.concatenate([chosen[0:1], chosen[1:2]], axis=1)
    row, lane = iota((128, 128), 0), iota((128, 128), 1)
    row_step = (row % 8) // 4
    natural = row_step * 64 + (row // 8) * 4 + row % 4
    chosen_at = jnp.sum(jnp.where(lane == natural, chosen, 0.0), axis=1, keepdims=True)
    before = (lane < natural) & (lane // 64 == row_step)
    rank = jnp.sum(jnp.where(before, chosen, 0.0), axis=1, keepdims=True).astype(jnp.int32)
    slot_at = rank + jnp.where(row_step == core, 0, CAP)
    picked = jnp.where((lane == slot_at) & (chosen_at > 0.5), 1.0, 0.0)
    spread[...] = picked.astype(BF16)
    pick[...] = jnp.transpose(picked)
    router_row = jnp.concatenate([router_v[...].astype(F32), jnp.zeros((1, 512 - W), F32)], axis=1)
    edge_row, edge_lane = iota((8, 512), 0), iota((8, 512), 1)
    edge[...] = jnp.where(
        edge_row == 0, router_row, jnp.where((edge_row == 1) & (edge_lane >= W) & (edge_lane < W + 2), 1.0, 0.0)
    ).astype(BF16)

    def padded(rows):
        return jnp.concatenate([rows, jnp.zeros((rows.shape[0], 512 - W), F32)], axis=1)

    l_resid.wait()
    l_gain.wait()
    owned = iota((8, 128), 0)
    owned = (owned // 4) * 64 + g_me * 4 + owned % 4 == iota((8, 128), 1)
    base_v[0:8] = padded(dot(jnp.where(owned, 1.0, 0.0).astype(BF16), resid_v[...].reshape(128, W)))
    base_v[8:16] = jnp.broadcast_to(padded(gain_v[...].astype(F32).reshape(1, W)), (8, 512))

    pl.semaphore_wait(barrier, len(ATTN_ORDER) + len(NEIGHBOURS))

    def spread_attn(phase, src_of, dst, slot):
        for step in ATTN_ORDER:
            peer = attn_peer(*step)
            remote(phase, src_of(peer), dst.at[slot], peer, slot, attn_id(peer)).start()

    def spread_group(phase, src_of, dst):
        for step in GROUP_ORDER:
            peer = group_peer(*step)
            remote(phase, src_of(peer), dst.at[g_me], peer, g_me, group_id(peer)).start()

    def await_all(phase, dst):
        every = dst.at[pl.ds(0, 15)]
        remote(phase, every, every, 0, 0, attn_id(me)).wait_recv()

    spread_attn(QUERY, lambda peer: tx1.at[peer], rx1, me)
    tell(0)

    l_pool.wait()
    l_mig.wait()
    l_t1.wait()
    l_pair.wait()
    t8 = jnp.concatenate([tab1[...], t2], axis=0)
    q32 = jnp.concatenate([q8[:, h * HD:(h + 1) * HD] for h in range(4)], axis=0)
    q32b = q32.astype(BF16)
    pair8 = jnp.concatenate([pair_v[0].astype(F32), pair_v[1].astype(F32)], axis=0)
    peak = jnp.full((32, 128), NONE, F32)
    all_counts = []
    for c in range(TOKENS // CHUNK):
        pages = CHUNK // PAGE
        count = counts(t8, len8, c * pages, CHUNK)
        count = jnp.concatenate([count] * 4, axis=0)
        s = dot_nt(q32b, pool[c * pages:(c + 1) * pages, :, 0:HD].reshape(CHUNK, HD)) * SCALE
        s = jnp.where(count > 0.5, s, NONE)
        score[0, :, c * CHUNK:(c + 1) * CHUNK] = s
        score[1, :, c * CHUNK:(c + 1) * CHUNK] = count
        for b in range(CHUNK // 128):
            peak = jnp.maximum(peak, s[:, b * 128:(b + 1) * 128])
    m_local = jnp.max(peak, axis=1, keepdims=True)
    sums = jnp.zeros((32, 128), F32)
    o_local = jnp.zeros((32, HD), F32)
    for c in range(TOKENS // CHUNK):
        count = score[1, :, c * CHUNK:(c + 1) * CHUNK]
        weight = jnp.where(count > 0.5, count * jnp.exp(score[0, :, c * CHUNK:(c + 1) * CHUNK] - m_local), 0.0)
        for b in range(CHUNK // 128):
            sums = sums + weight[:, b * 128:(b + 1) * 128]
        pages = CHUNK // PAGE
        o_local = o_local + dot(
            weight.astype(BF16), pool[c * pages:(c + 1) * pages, :, HD:2 * HD].reshape(CHUNK, HD)
        )
    l_local = jnp.sum(sums, axis=1, keepdims=True)
    key32 = jnp.concatenate([pair8[:, 0:HD]] * 4, axis=0)
    value32 = jnp.concatenate([pair8[:, HD:2 * HD]] * 4, axis=0)
    own_score = jnp.sum(q32 * key32, axis=1, keepdims=True) * SCALE

    for dx in (2, 1, 3, 0):
        if dx == 1:
            hear(0)
            tell(1)
        steps = [(dx, dy, dc) for dy in (0, 1) for dc in (0, 1)]
        sources = [attn_peer(*step) for step in steps]
        for step, source in zip(steps, sources):
            if step != (0, 0, 0):
                remote(QUERY, tx1.at[source], rx1.at[source], source, source, attn_id(me)).wait_recv()
        pages = [migrations[0, source] for source in sources]
        asked = [rx1[source] for source in sources]
        count = jnp.concatenate([a[:, HD:HD + PAGE].astype(F32) for a in asked], axis=0)
        s = jnp.concatenate([dot_nt(a[:, 0:HD], pool[page, :, 0:HD]) for a, page in zip(asked, pages)], axis=0) * SCALE
        live = count > 0.5
        top = jnp.max(jnp.where(live, s, NONE), axis=1, keepdims=True).astype(BF16).astype(F32)
        weight = jnp.where(live, count * jnp.exp(s - top), 0.0)
        total = jnp.sum(weight, axis=1, keepdims=True)
        high = total.astype(BF16).astype(F32)
        at = iota((64, 128), 1)
        stat = jnp.where(at == 0, top, jnp.where(at == 1, high, jnp.where(at == 2, total - high, 0.0))).astype(BF16)
        weight = weight.astype(BF16)
        for i, (step, source) in enumerate(zip(steps, sources)):
            tx2[source, :, 0:HD] = dot(weight[16 * i:16 * i + 16], pool[pages[i], :, HD:2 * HD]).astype(BF16)
            tx2[source, :, HD:384] = stat[16 * i:16 * i + 16]
        for step, source in zip(steps, sources):
            if step != (0, 0, 0):
                remote(PARTIAL, tx2.at[source], rx2.at[me], source, me, attn_id(source)).start()
    rx2[me] = tx2[me]
    hear(1)
    tell(2)

    def of_step(rows, i):
        return jnp.concatenate([rows[8 * h + 4 * i:8 * h + 4 * i + 4] for h in range(4)], axis=0)

    top = jnp.maximum(m_local, own_score)
    f_local, f_own = jnp.exp(m_local - top), jnp.exp(own_score - top)
    above = f_local * o_local + f_own.astype(BF16).astype(F32) * value32
    first_step = of_step(above / (f_local * l_local + f_own), 0).astype(BF16)
    tx3[0] = first_step
    rx3[0, me] = first_step
    spread_attn(HEADS_FIRST, lambda peer: tx3.at[0], rx3.at[0], me)

    await_all(PARTIAL, rx2)
    back = rx2[...].astype(F32)
    m_s = back[:, :, HD:HD + 1]
    l_s = back[:, :, HD + 1:HD + 2] + back[:, :, HD + 2:HD + 3]
    m_r = jnp.max(m_s, axis=0)
    w_s = jnp.exp(m_s - m_r[None])
    l_r = jnp.sum(w_s * l_s, axis=0)
    o_r = jnp.sum(w_s * back[:, :, 0:HD], axis=0)
    m_near, l_near, o_near = of_step(m_local, 1), of_step(l_local, 1), of_step(o_local, 1)
    own_near = of_step(own_score, 1)
    top = jnp.maximum(jnp.maximum(m_near, m_r), own_near)
    f_near, f_far, f_own = jnp.exp(m_near - top), jnp.exp(m_r - top), jnp.exp(own_near - top)
    below = f_near * l_near + f_far * l_r + f_own
    above = f_near * o_near + f_far * o_r + f_own.astype(BF16).astype(F32) * of_step(value32, 1)
    second_step = (above / below).astype(BF16)
    tx3[1] = second_step
    rx3[1, me] = second_step
    spread_attn(HEADS_OUT, lambda peer: tx3.at[1], rx3.at[1], me)
    hear(2)
    tell(3)
    l_wo.wait()
    await_all(HEADS_FIRST, rx3.at[0])
    await_all(HEADS_OUT, rx3.at[1])

    steps = [rx3[i].astype(F32).reshape(NA, 2, 8, HD) for i in range(2)]
    turned = [jnp.concatenate([t[:, :, 4:8], t[:, :, 0:4]], axis=2) for t in steps]
    upper = iota((NA, 2, 8, HD), 2) < 4
    x = [
        jnp.where(upper, steps[0], turned[1]).astype(BF16),
        jnp.where(upper, turned[0], steps[1]).astype(BF16),
    ]
    partial = jnp.zeros((128, W), F32)
    for h in range(4):
        partial = partial + dot_nt(x[h % 2][:, h // 2].reshape(128, HD), wo[:, h * HD:(h + 1) * HD])

    tx4[...] = fold(padded(partial).reshape(NG, 8, 512)).astype(BF16)
    rx4[g_me] = tx4[g_me]
    hear(3)
    spread_group(PROJ, lambda peer: tx4.at[peer], rx4)

    await_all(PROJ, rx4)
    hidden = base_v[0:8] + unfold(jnp.sum(rx4[...].astype(F32), axis=0))
    hidden_v[...] = hidden
    squares = jnp.sum(hidden * hidden, axis=1, keepdims=True)
    high = squares.astype(BF16).astype(F32)
    scaled = hidden * base_v[8:16]
    scaled = jnp.where(edge_lane == W, high, jnp.where(edge_lane == W + 1, squares - high, scaled))
    scaled = fold(scaled).astype(BF16)
    tx5[...] = scaled
    rx5[g_me] = scaled
    spread_group(ROWS_IN, lambda peer: tx5, rx5)
    await_all(ROWS_IN, rx5)

    rows = unfold(rx5[...].astype(F32)).reshape(128, 512).astype(BF16)
    rows_v[...] = rows
    stats = dot_nt(edge[...], rows)
    tx6[...] = stats
    rx6[me] = stats
    spread_attn(STATS, lambda peer: tx6, rx6, me)
    slots_v[...] = dot(pick[0:2 * CAP, :].astype(BF16), rows_v[:, 0:W]).astype(BF16)

    l_wg.wait()
    l_wu.wait()
    left = iota((2 * CAP, 128), 1) < 64

    def compute_pair(p):
        lanes = pl.ds(pl.multiple_of(640 * p, 128), 640)
        g = dot(slots_v[...], wg[:, lanes])
        u = dot(slots_v[...], wu[:, lanes])
        g2, u2 = g[:, 256:384], pltpu.roll(u[:, 256:384], 64, axis=1)
        pieces = (
            (g[:, 0:128], u[:, 0:128], jnp.where(left, g2, u2), g[:, 128:256], u[:, 128:256]),
            (g[:, 384:512], u[:, 384:512], jnp.where(left, u2, g2), g[:, 512:640], u[:, 512:640]),
        )
        for i in range(2):
            piece = jnp.concatenate(pieces[i], axis=1)
            j = 2 * p + i
            own_v[j] = piece[0:CAP]
            txs[j] = piece[CAP:2 * CAP].astype(BF16)
            remote(SIBLING, txs.at[j], rxs.at[j], j, j, attn_id(sibling)).start()

    def reduce_pair(dx):
        for dy in (1, 0):
            j = chip_peer(dx, dy)
            remote(SIBLING, txs.at[j], rxs.at[j], j, j, attn_id(sibling)).wait_recv()
            both = (own_v[j] + rxs[j].astype(F32)).astype(BF16)
            tx7[j] = both[:, 0:384]
            tx7b[j] = both[:, 384:640]
            if (dx, dy) != (0, 0):
                remote(REDUCE, tx7.at[j], rx7.at[chip], j, chip, attn_id(2 * j + core)).start()

    far_first = (2, 1, 3, 0)
    for k, dx in enumerate(far_first):
        compute_pair(lax.rem(at_x + dx, 4))
        if k > 0:
            reduce_pair(far_first[k - 1])
    reduce_pair(0)

    def to_chips(phase, src_of, dst):
        for step in CHIP_ORDER:
            j = chip_peer(*step)
            remote(phase, src_of(j), dst, j, chip, attn_id(2 * j + core)).start()

    to_chips(REDUCE_B, lambda j: tx7b.at[j], rx7b.at[chip])

    await_all(STATS, rx6)
    stats = jnp.sum(rx6[...], axis=0)
    inverse_row = lax.rsqrt(stats[1:2] / D + EPSILON)
    route_row = 1.0 / (1.0 + jnp.exp(-(stats[0:1] * inverse_row)))
    picked = pick[0:2 * CAP, :]
    inverse = jnp.sum(picked[0:CAP] * inverse_row, axis=1, keepdims=True)
    route = jnp.sum(picked * route_row, axis=1, keepdims=True)

    def summed(phase, mine, theirs):
        total = mine[chip].astype(F32)
        for step in reversed(CHIP_ORDER):
            j = chip_peer(*step)
            remote(phase, mine.at[j], theirs.at[j], j, j, attn_id(me)).wait_recv()
            total = total + theirs[j].astype(F32)
        return total * inverse

    total = summed(REDUCE, tx7, rx7)
    mixed = total[:, 256:384]
    half = silu(mixed) * pltpu.roll(mixed, 64, axis=1)
    right = jnp.where(iota((CAP, 128), 1) < 64, 0, 1)
    half = jnp.where(right == lax.rem(chip, 2), half, 0.0)
    activated = jnp.concatenate([silu(total[:, 0:128]) * total[:, 128:256], half], axis=1).astype(BF16)
    tx8[...] = activated
    rx8[0, chip] = activated
    to_chips(ACT, lambda j: tx8, rx8.at[0, chip])
    remote(FORWARD, tx8, rx8.at[1, chip], chip, chip, attn_id(sibling)).start()
    total = summed(REDUCE_B, tx7b, rx7b)
    activated = (silu(total[:, 0:128]) * total[:, 128:256]).astype(BF16)
    tx8b[...] = activated
    rx8b[0, chip] = activated
    to_chips(ACT_B, lambda j: tx8b, rx8b.at[0, chip])
    remote(FORWARD_B, tx8b, rx8b.at[1, chip], chip, chip, attn_id(sibling)).start()
    l_wd.wait()

    def forward_pair(dx, phase, onward, src, dst):
        for dy in (0, 1):
            if (dx, dy) != (0, 0):
                j = chip_peer(dx, dy)
                remote(phase, src, dst.at[0, j], j, j, attn_id(me)).wait_recv()
                remote(onward, dst.at[0, j], dst.at[1, j], j, j, attn_id(sibling)).start()

    def down_pair(dx):
        p = lax.rem(at_x + dx, 4)
        for j in (2 * p, 2 * p + 1):
            remote(FORWARD, tx8, rx8.at[1, j], j, j, attn_id(me)).wait_recv()
            remote(FORWARD_B, tx8b, rx8b.at[1, j], j, j, attn_id(me)).wait_recv()
        parts = []
        for side in range(2):
            a, b = rx8[side, 2 * p], rx8[side, 2 * p + 1]
            middle = (a[:, 128:256].astype(F32) + b[:, 128:256].astype(F32)).astype(BF16)
            parts.append(jnp.concatenate(
                [a[:, 0:128], rx8b[side, 2 * p], middle, b[:, 0:128], rx8b[side, 2 * p + 1]], axis=1
            ))
        lanes = pl.ds(pl.multiple_of(640 * p, 128), 640)
        return dot_nt(jnp.concatenate(parts, axis=0), wd[:, lanes])

    result = jnp.zeros((2 * CAP, W), F32)
    for dx in far_first:
        forward_pair(dx, ACT, FORWARD, tx8, rx8)
    for k, dx in enumerate(far_first):
        forward_pair(dx, ACT_B, FORWARD_B, tx8b, rx8b)
        if k > 0:
            result = result + down_pair(far_first[k - 1])
    result = result + down_pair(0)
    result = (result * route).astype(BF16)
    added = dot(spread[:, 0:2 * CAP], result)
    tx9[...] = fold(padded(added).reshape(NG, 8, 512)).astype(BF16)
    rx9[g_me] = tx9[g_me]
    spread_group(BACK, lambda peer: tx9.at[peer], rx9)

    def sent(phase, every):
        remote(phase, every, every, 0, 0, attn_id(me)).wait_send()

    for phase, dst in ((QUERY, rx1), (PARTIAL, rx2), (HEADS_FIRST, rx3.at[0]), (HEADS_OUT, rx3.at[1]), (PROJ, rx4), (ROWS_IN, rx5), (STATS, rx6), (BACK, rx9)):
        sent(phase, dst.at[pl.ds(0, 15)])
    sent(SIBLING, txs)
    sent(REDUCE, tx7.at[pl.ds(0, CHIPS - 1)])
    sent(ACT, rx8.at[0, pl.ds(0, CHIPS - 1)])
    sent(FORWARD, rx8.at[0])
    sent(REDUCE_B, tx7b.at[pl.ds(0, CHIPS - 1)])
    sent(ACT_B, rx8b.at[0, pl.ds(0, CHIPS - 1)])
    sent(FORWARD_B, rx8b.at[0])
    await_all(BACK, rx9)
    final = hidden_v[...] + unfold(jnp.sum(rx9[...].astype(F32), axis=0))
    out[0] = final[0:4, 0:W].astype(BF16)
    out[1] = final[4:8, 0:W].astype(BF16)


def on_device(
    queries, new_pairs, kv_pool, table_first, table_second, lengths, migrations, residual,
    out_proj, norm_gain, router, routes, gate_weight, up_weight, down_weight,
):
    vmem, smem = pltpu.VMEM, pltpu.SMEM
    return pl.pallas_call(
        body,
        out_shape=jax.ShapeDtypeStruct((2, 4, W), BF16),
        in_specs=[pl.BlockSpec(memory_space=pltpu.HBM)] * 15,
        out_specs=pl.BlockSpec(memory_space=pltpu.VMEM),
        scratch_shapes=[
            smem((2, 4), jnp.int32), smem((1, 16), jnp.int32),
            vmem((2, 4, 1024), BF16), vmem((2, 4, 512), BF16), vmem((LOCAL, PAGE, 2 * HD), BF16),
            vmem((4, 16), jnp.int32), vmem((4, 16), jnp.int32), vmem((2, 64, W), BF16), vmem((W, 1024), BF16),
            vmem((W,), BF16), vmem((1, W), BF16), vmem((3, 2, 64), jnp.int32),
            vmem((W, 2560), BF16), vmem((W, 2560), BF16), vmem((W, 2560), BF16),
            pltpu.SemaphoreType.DMA((15,)), pltpu.SemaphoreType.DMA((15,)), pltpu.SemaphoreType.DMA((15, 16)), pltpu.SemaphoreType.REGULAR((4,)),
            vmem((NA, 16, 384), BF16), vmem((NA, 16, 384), BF16),
            vmem((NA, 16, 384), BF16), vmem((NA, 16, 384), BF16),
            vmem((2, 16, HD), BF16), vmem((2, NA, 16, HD), BF16),
            vmem((NG, 16, 256), BF16), vmem((NG, 16, 256), BF16),
            vmem((16, 256), BF16), vmem((NG, 16, 256), BF16),
            vmem((8, 128), F32), vmem((NA, 8, 128), F32),
            vmem((CHIPS, CAP, 640), BF16), vmem((CHIPS, CAP, 640), BF16),
            vmem((CHIPS, CAP, 384), BF16), vmem((CHIPS, CAP, 384), BF16),
            vmem((CHIPS, CAP, 256), BF16), vmem((CHIPS, CAP, 256), BF16),
            vmem((CAP, 256), BF16), vmem((2, CHIPS, CAP, 256), BF16),
            vmem((CAP, 128), BF16), vmem((2, CHIPS, CAP, 128), BF16),
            vmem((NG, 16, 256), BF16), vmem((NG, 16, 256), BF16),
            vmem((2, 32, TOKENS), F32), vmem((16, 512), F32), vmem((8, 512), F32), vmem((2 * CAP, W), BF16), vmem((128, 512), BF16),
            vmem((128, 128), F32), vmem((128, 128), BF16), vmem((8, 512), BF16), vmem((CHIPS, CAP, 640), F32),
        ],
        compiler_params=pltpu.CompilerParams(
            collective_id=0, has_side_effects=True, vmem_limit_bytes=60 * 1024 * 1024
        ),
        name="layer",
    )(
        queries, new_pairs, kv_pool, table_first, table_second, lengths, migrations, residual,
        out_proj.T, norm_gain, router.T, routes.transpose(2, 0, 1), gate_weight, up_weight, down_weight[0].T,
    )


def solution(mesh):
    return jax.shard_map(
        on_device,
        mesh=mesh,
        in_specs=(
            P(None, "attn", ("ffn", "tp")),
            P(None, "attn", None),
            P("attn", None, None),
            P("attn", None),
            P("attn", None),
            P(None, "attn"),
            P("attn", None),
            P(None, None, "attn"),
            P(("ffn", "tp"), "attn"),
            P("attn"),
            P("attn", "ffn"),
            P(),
            P("ffn", "attn", "tp"),
            P("ffn", "attn", "tp"),
            P("ffn", "tp", "attn"),
        ),
        out_specs=P(None, ("ffn", "tp"), "attn"),
        check_vma=False,
    )
```

```python
import jax
import jax.numpy as jnp
from jax import lax
from jax.experimental import pallas as pl
from jax.experimental.pallas import tpu as pltpu
from jax.sharding import PartitionSpec as P

F32, BF16 = jnp.float32, jnp.bfloat16
MESH = pl.DeviceIdType.MESH
D = 7168
EPSILON = 1e-6
NA, NG = 16, 16
CHIPS = 8
LOCAL = 48
PAGE, HD = 64, 256
TOKENS = LOCAL * PAGE
CHUNK = 512
CAP = 48
W = 448
NONE = -1e30
SCALE = HD ** -0.5
NT_DIMS = (((1,), (1,)), ((), ()))
ATTN_ORDER = [(dx, dy, dc) for dx in (2, 1, 3, 0) for dy in (1, 0) for dc in (0, 1) if (dx, dy, dc) != (0, 0, 0)]
GROUP_ORDER = [(dz, dt) for dt in (1, 0) for dz in (4, 3, 5, 2, 6, 1, 7, 0) if (dz, dt) != (0, 0)]
NEIGHBOURS = [(0, 1), (1, 0), (7, 0)]
NEAR_FIRST = (0, 1, 3, 2)
CHIP_ORDER = [(dx, dy) for dx in (2, 1, 3, 0) for dy in (1, 0) if (dx, dy) != (0, 0)]
QUERY, PARTIAL, HEADS_OUT, PROJ, ROWS_IN, STATS, SIBLING, REDUCE, ACT, FORWARD, BACK, HEADS_FIRST, REDUCE_B, ACT_B, FORWARD_B = range(15)
TOGETHER = (PARTIAL, HEADS_OUT, PROJ, ROWS_IN, STATS, BACK, HEADS_FIRST)


def iota(shape, axis):
    return lax.broadcasted_iota(jnp.int32, shape, axis)


def dot(a, b):
    return jnp.dot(a, b, preferred_element_type=F32)


def dot_nt(a, b):
    return lax.dot_general(a, b, NT_DIMS, preferred_element_type=F32)


def fold(block):
    return jnp.concatenate([block[..., :256], block[..., 256:]], axis=-2)


def unfold(block):
    return jnp.concatenate([block[..., :8, :], block[..., 8:, :]], axis=-1)


def silu(v):
    return v / (1.0 + jnp.exp(-v))


def body(
    queries, new_pairs, kv_pool, table_first, table_second, lengths_in, migrations_in, residual,
    out_proj, norm_gain, router, routes, gate_weight, up_weight, down_weight,
    out,
    lengths, migrations, q_v, pair_v, pool, tab1, tab2, resid_v, wo, gain_v, router_v, routes_v, wg, wu, wd,
    load_sem, send, recv, gossip,
    tx1, rx1, tx2, rx2, tx3, rx3, tx4, rx4, tx5, rx5, tx6, rx6, txs, rxs, tx7, rx7, tx7b, rx7b, tx8, rx8, tx8b, rx8b, tx9, rx9,
    score, base_v, hidden_v, slots_v, rows_v, pick, spread, edge, own_v,
):
    me = lax.axis_index("attn")
    expert = lax.axis_index("ffn")
    g_me = expert * 2 + lax.axis_index("tp")
    core = lax.rem(me, 2)
    chip = me // 2
    sibling = me + 1 - 2 * core
    at_x, at_y = me // 4, lax.rem(chip, 2)
    at_t = lax.rem(g_me, 2)

    def attn_peer(dx, dy, dc):
        return lax.rem(at_x + dx, 4) * 4 + lax.rem(at_y + dy, 2) * 2 + lax.rem(core + dc, 2)

    def chip_peer(dx, dy):
        return lax.rem(at_x + dx, 4) * 2 + lax.rem(at_y + dy, 2)

    def group_peer(dz, dt):
        return lax.rem(expert + dz, 8) * 2 + lax.rem(at_t + dt, 2)

    pairs = [
        (queries, q_v), (table_second, tab2), (table_first, tab1), (new_pairs, pair_v),
        (lengths_in, lengths), (migrations_in, migrations),
        (kv_pool.at[pl.ds(0, LOCAL)], pool), (routes, routes_v), (router, router_v), (norm_gain, gain_v),
        (residual, resid_v), (out_proj, wo), (gate_weight.at[0], wg), (up_weight.at[0], wu), (down_weight, wd),
    ]
    loads = [pltpu.make_async_copy(src, dst, load_sem.at[i]) for i, (src, dst) in enumerate(pairs)]
    for load in loads:
        load.start()
    (l_q, l_t2, l_t1, l_pair, l_len, l_mig, l_pool, l_routes, l_router, l_gain, l_resid, l_wo, l_wg, l_wu, l_wd) = loads

    def attn_id(i):
        return {"attn": i}

    def group_id(g):
        return {"ffn": g // 2, "tp": lax.rem(g, 2)}

    barrier = pltpu.get_barrier_semaphore()

    for step in ATTN_ORDER:
        pl.semaphore_signal(barrier, inc=1, device_id=attn_id(attn_peer(*step)), device_id_type=MESH)
    for step in NEIGHBOURS:
        pl.semaphore_signal(barrier, inc=1, device_id=group_id(group_peer(*step)), device_id_type=MESH)

    def tell(i):
        for dz in (1, 7):
            pl.semaphore_signal(gossip.at[i], inc=1, device_id=group_id(group_peer(dz, 0)), device_id_type=MESH)

    def hear(i):
        pl.semaphore_wait(gossip.at[i], 2)

    def remote(phase, src, dst, slot_to, slot_from, device):
        return pltpu.make_async_remote_copy(
            src_ref=src, dst_ref=dst, send_sem=send.at[phase], recv_sem=recv.at[phase, 0 if phase in TOGETHER else slot_from],
            device_id=device, device_id_type=MESH,
        )

    l_q.wait()
    l_t2.wait()
    l_len.wait()
    q8 = jnp.concatenate([q_v[0].astype(F32), q_v[1].astype(F32)], axis=0)
    t2 = tab2[...]
    t2x = jnp.concatenate([t2, t2, t2, t2], axis=0)

    def column(rows, values):
        at = iota((rows, 1), 0)
        result = jnp.zeros((rows, 1), jnp.int32)
        for i in range(rows):
            result = jnp.where(at == i, values[i], result)
        return result

    len2 = column(16, [lengths[1, i % 4] for i in range(16)])
    len8 = column(8, [lengths[i // 4, i % 4] for i in range(8)])

    def counts(table, length, first, width):
        lane = iota((table.shape[0], width), 1)
        page, place = first + lane // PAGE, lane % PAGE
        total = jnp.zeros((table.shape[0], width), F32)
        for k in range(16):
            left = length - k * PAGE
            total = total + jnp.where((page == table[:, k:k + 1]) & (place < left), 1.0, 0.0)
        return total

    q2 = jnp.concatenate([q8[4:8, h * HD:(h + 1) * HD] for h in range(4)], axis=0).astype(BF16)
    for s in range(0, NA, 2):
        c = counts(t2x, len2, LOCAL + s, 2 * PAGE)
        tx1[s, :, 0:HD] = q2
        tx1[s, :, HD:384] = c.astype(BF16)
        tx1[s + 1, :, 0:HD] = q2
        tx1[s + 1, :, HD:384] = pltpu.roll(c, PAGE, axis=1).astype(BF16)
    rx1[me] = tx1[me]

    l_routes.wait()
    l_router.wait()
    named = [routes_v[i] == expert for i in range(3)]
    chosen = jnp.where(named[0] | named[1] | named[2], 1.0, 0.0)
    chosen = jnp.concatenate([chosen[0:1], chosen[1:2]], axis=1)
    row, lane = iota((128, 128), 0), iota((128, 128), 1)
    row_step = (row % 8) // 4
    natural = row_step * 64 + (row // 8) * 4 + row % 4
    chosen_at = jnp.sum(jnp.where(lane == natural, chosen, 0.0), axis=1, keepdims=True)
    before = (lane < natural) & (lane // 64 == row_step)
    rank = jnp.sum(jnp.where(before, chosen, 0.0), axis=1, keepdims=True).astype(jnp.int32)
    slot_at = rank + jnp.where(row_step == core, 0, CAP)
    picked = jnp.where((lane == slot_at) & (chosen_at > 0.5), 1.0, 0.0)
    spread[...] = picked.astype(BF16)
    pick[...] = jnp.transpose(picked)
    router_row = jnp.concatenate([router_v[...].astype(F32), jnp.zeros((1, 512 - W), F32)], axis=1)
    edge_row, edge_lane = iota((8, 512), 0), iota((8, 512), 1)
    edge[...] = jnp.where(
        edge_row == 0, router_row, jnp.where((edge_row == 1) & (edge_lane >= W) & (edge_lane < W + 2), 1.0, 0.0)
    ).astype(BF16)

    def padded(rows):
        return jnp.concatenate([rows, jnp.zeros((rows.shape[0], 512 - W), F32)], axis=1)

    l_resid.wait()
    l_gain.wait()
    owned = iota((8, 128), 0)
    owned = (owned // 4) * 64 + g_me * 4 + owned % 4 == iota((8, 128), 1)
    base_v[0:8] = padded(dot(jnp.where(owned, 1.0, 0.0).astype(BF16), resid_v[...].reshape(128, W)))
    base_v[8:16] = jnp.broadcast_to(padded(gain_v[...].astype(F32).reshape(1, W)), (8, 512))

    pl.semaphore_wait(barrier, len(ATTN_ORDER) + len(NEIGHBOURS))

    def spread_attn(phase, src_of, dst, slot):
        for step in ATTN_ORDER:
            peer = attn_peer(*step)
            remote(phase, src_of(peer), dst.at[slot], peer, slot, attn_id(peer)).start()

    def spread_group(phase, src_of, dst):
        for step in GROUP_ORDER:
            peer = group_peer(*step)
            remote(phase, src_of(peer), dst.at[g_me], peer, g_me, group_id(peer)).start()

    def await_all(phase, dst):
        every = dst.at[pl.ds(0, 15)]
        remote(phase, every, every, 0, 0, attn_id(me)).wait_recv()

    spread_attn(QUERY, lambda peer: tx1.at[peer], rx1, me)
    tell(0)

    l_pool.wait()
    l_mig.wait()
    l_t1.wait()
    l_pair.wait()
    t8 = jnp.concatenate([tab1[...], t2], axis=0)
    q32 = jnp.concatenate([q8[:, h * HD:(h + 1) * HD] for h in range(4)], axis=0)
    q32b = q32.astype(BF16)
    pair8 = jnp.concatenate([pair_v[0].astype(F32), pair_v[1].astype(F32)], axis=0)
    peak = jnp.full((32, 128), NONE, F32)
    all_counts = []
    for c in range(TOKENS // CHUNK):
        pages = CHUNK // PAGE
        count = counts(t8, len8, c * pages, CHUNK)
        count = jnp.concatenate([count] * 4, axis=0)
        s = dot_nt(q32b, pool[c * pages:(c + 1) * pages, :, 0:HD].reshape(CHUNK, HD)) * SCALE
        s = jnp.where(count > 0.5, s, NONE)
        score[0, :, c * CHUNK:(c + 1) * CHUNK] = s
        score[1, :, c * CHUNK:(c + 1) * CHUNK] = count
        for b in range(CHUNK // 128):
            peak = jnp.maximum(peak, s[:, b * 128:(b + 1) * 128])
    m_local = jnp.max(peak, axis=1, keepdims=True)
    sums = jnp.zeros((32, 128), F32)
    o_local = jnp.zeros((32, HD), F32)
    for c in range(TOKENS // CHUNK):
        count = score[1, :, c * CHUNK:(c + 1) * CHUNK]
        weight = jnp.where(count > 0.5, count * jnp.exp(score[0, :, c * CHUNK:(c + 1) * CHUNK] - m_local), 0.0)
        for b in range(CHUNK // 128):
            sums = sums + weight[:, b * 128:(b + 1) * 128]
        pages = CHUNK // PAGE
        o_local = o_local + dot(
            weight.astype(BF16), pool[c * pages:(c + 1) * pages, :, HD:2 * HD].reshape(CHUNK, HD)
        )
    l_local = jnp.sum(sums, axis=1, keepdims=True)
    key32 = jnp.concatenate([pair8[:, 0:HD]] * 4, axis=0)
    value32 = jnp.concatenate([pair8[:, HD:2 * HD]] * 4, axis=0)
    own_score = jnp.sum(q32 * key32, axis=1, keepdims=True) * SCALE

    for dx in (2, 1, 3, 0):
        if dx == 1:
            hear(0)
            tell(1)
        steps = [(dx, dy, dc) for dy in (0, 1) for dc in (0, 1)]
        sources = [attn_peer(*step) for step in steps]
        for step, source in zip(steps, sources):
            if step != (0, 0, 0):
                remote(QUERY, tx1.at[source], rx1.at[source], source, source, attn_id(me)).wait_recv()
        pages = [migrations[0, source] for source in sources]
        asked = [rx1[source] for source in sources]
        count = jnp.concatenate([a[:, HD:HD + PAGE].astype(F32) for a in asked], axis=0)
        s = jnp.concatenate([dot_nt(a[:, 0:HD], pool[page, :, 0:HD]) for a, page in zip(asked, pages)], axis=0) * SCALE
        live = count > 0.5
        top = jnp.max(jnp.where(live, s, NONE), axis=1, keepdims=True).astype(BF16).astype(F32)
        weight = jnp.where(live, count * jnp.exp(s - top), 0.0)
        total = jnp.sum(weight, axis=1, keepdims=True)
        high = total.astype(BF16).astype(F32)
        at = iota((64, 128), 1)
        stat = jnp.where(at == 0, top, jnp.where(at == 1, high, jnp.where(at == 2, total - high, 0.0))).astype(BF16)
        weight = weight.astype(BF16)
        for i, (step, source) in enumerate(zip(steps, sources)):
            tx2[source, :, 0:HD] = dot(weight[16 * i:16 * i + 16], pool[pages[i], :, HD:2 * HD]).astype(BF16)
            tx2[source, :, HD:384] = stat[16 * i:16 * i + 16]
        for step, source in zip(steps, sources):
            if step != (0, 0, 0):
                remote(PARTIAL, tx2.at[source], rx2.at[me], source, me, attn_id(source)).start()
    rx2[me] = tx2[me]
    hear(1)
    tell(2)

    def of_step(rows, i):
        return jnp.concatenate([rows[8 * h + 4 * i:8 * h + 4 * i + 4] for h in range(4)], axis=0)

    top = jnp.maximum(m_local, own_score)
    f_local, f_own = jnp.exp(m_local - top), jnp.exp(own_score - top)
    above = f_local * o_local + f_own.astype(BF16).astype(F32) * value32
    first_step = of_step(above / (f_local * l_local + f_own), 0).astype(BF16)
    tx3[0] = first_step
    rx3[0, me] = first_step
    spread_attn(HEADS_FIRST, lambda peer: tx3.at[0], rx3.at[0], me)

    await_all(PARTIAL, rx2)
    back = rx2[...].astype(F32)
    m_s = back[:, :, HD:HD + 1]
    l_s = back[:, :, HD + 1:HD + 2] + back[:, :, HD + 2:HD + 3]
    m_r = jnp.max(m_s, axis=0)
    w_s = jnp.exp(m_s - m_r[None])
    l_r = jnp.sum(w_s * l_s, axis=0)
    o_r = jnp.sum(w_s * back[:, :, 0:HD], axis=0)
    m_near, l_near, o_near = of_step(m_local, 1), of_step(l_local, 1), of_step(o_local, 1)
    own_near = of_step(own_score, 1)
    top = jnp.maximum(jnp.maximum(m_near, m_r), own_near)
    f_near, f_far, f_own = jnp.exp(m_near - top), jnp.exp(m_r - top), jnp.exp(own_near - top)
    below = f_near * l_near + f_far * l_r + f_own
    above = f_near * o_near + f_far * o_r + f_own.astype(BF16).astype(F32) * of_step(value32, 1)
    second_step = (above / below).astype(BF16)
    tx3[1] = second_step
    rx3[1, me] = second_step
    spread_attn(HEADS_OUT, lambda peer: tx3.at[1], rx3.at[1], me)
    hear(2)
    tell(3)
    l_wo.wait()
    await_all(HEADS_FIRST, rx3.at[0])
    await_all(HEADS_OUT, rx3.at[1])

    steps = [rx3[i].astype(F32).reshape(NA, 2, 8, HD) for i in range(2)]
    turned = [jnp.concatenate([t[:, :, 4:8], t[:, :, 0:4]], axis=2) for t in steps]
    upper = iota((NA, 2, 8, HD), 2) < 4
    x = [
        jnp.where(upper, steps[0], turned[1]).astype(BF16),
        jnp.where(upper, turned[0], steps[1]).astype(BF16),
    ]
    partial = jnp.zeros((128, W), F32)
    for h in range(4):
        partial = partial + dot_nt(x[h % 2][:, h // 2].reshape(128, HD), wo[:, h * HD:(h + 1) * HD])

    tx4[...] = fold(padded(partial).reshape(NG, 8, 512)).astype(BF16)
    rx4[g_me] = tx4[g_me]
    hear(3)
    spread_group(PROJ, lambda peer: tx4.at[peer], rx4)

    await_all(PROJ, rx4)
    hidden = base_v[0:8] + unfold(jnp.sum(rx4[...].astype(F32), axis=0))
    hidden_v[...] = hidden
    squares = jnp.sum(hidden * hidden, axis=1, keepdims=True)
    high = squares.astype(BF16).astype(F32)
    scaled = hidden * base_v[8:16]
    scaled = jnp.where(edge_lane == W, high, jnp.where(edge_lane == W + 1, squares - high, scaled))
    scaled = fold(scaled).astype(BF16)
    tx5[...] = scaled
    rx5[g_me] = scaled
    spread_group(ROWS_IN, lambda peer: tx5, rx5)
    await_all(ROWS_IN, rx5)

    rows = unfold(rx5[...].astype(F32)).reshape(128, 512).astype(BF16)
    rows_v[...] = rows
    stats = dot_nt(edge[...], rows)
    tx6[...] = stats
    rx6[me] = stats
    spread_attn(STATS, lambda peer: tx6, rx6, me)
    slots_v[...] = dot(pick[0:2 * CAP, :].astype(BF16), rows_v[:, 0:W]).astype(BF16)

    l_wg.wait()
    l_wu.wait()
    left = iota((2 * CAP, 128), 1) < 64

    def compute_pair(p):
        lanes = pl.ds(pl.multiple_of(640 * p, 128), 640)
        g = dot(slots_v[...], wg[:, lanes])
        u = dot(slots_v[...], wu[:, lanes])
        g2, u2 = g[:, 256:384], pltpu.roll(u[:, 256:384], 64, axis=1)
        pieces = (
            (g[:, 0:128], u[:, 0:128], jnp.where(left, g2, u2), g[:, 128:256], u[:, 128:256]),
            (g[:, 384:512], u[:, 384:512], jnp.where(left, u2, g2), g[:, 512:640], u[:, 512:640]),
        )
        for i in range(2):
            piece = jnp.concatenate(pieces[i], axis=1)
            j = 2 * p + i
            own_v[j] = piece[0:CAP]
            txs[j] = piece[CAP:2 * CAP].astype(BF16)
            remote(SIBLING, txs.at[j], rxs.at[j], j, j, attn_id(sibling)).start()

    def reduce_pair(dx):
        for dy in (1, 0):
            j = chip_peer(dx, dy)
            remote(SIBLING, txs.at[j], rxs.at[j], j, j, attn_id(sibling)).wait_recv()
            both = (own_v[j] + rxs[j].astype(F32)).astype(BF16)
            tx7[j] = both[:, 0:384]
            tx7b[j] = both[:, 384:640]
            if (dx, dy) != (0, 0):
                remote(REDUCE, tx7.at[j], rx7.at[chip], j, chip, attn_id(2 * j + core)).start()

    def send_second(dx):
        for dy in (1, 0):
            if (dx, dy) != (0, 0):
                j = chip_peer(dx, dy)
                remote(REDUCE_B, tx7b.at[j], rx7b.at[chip], j, chip, attn_id(2 * j + core)).start()

    far_first = (2, 1, 3, 0)
    for k, dx in enumerate(far_first):
        compute_pair(lax.rem(at_x + dx, 4))
        if k > 0:
            reduce_pair(far_first[k - 1])
        if k > 1:
            send_second(far_first[k - 2])
    reduce_pair(0)

    def to_chips(phase, src_of, dst):
        for step in CHIP_ORDER:
            j = chip_peer(*step)
            remote(phase, src_of(j), dst, j, chip, attn_id(2 * j + core)).start()

    send_second(far_first[2])
    send_second(0)

    await_all(STATS, rx6)
    stats = jnp.sum(rx6[...], axis=0)
    inverse_row = lax.rsqrt(stats[1:2] / D + EPSILON)
    route_row = 1.0 / (1.0 + jnp.exp(-(stats[0:1] * inverse_row)))
    picked = pick[0:2 * CAP, :]
    inverse = jnp.sum(picked[0:CAP] * inverse_row, axis=1, keepdims=True)
    route = jnp.sum(picked * route_row, axis=1, keepdims=True)

    def summed(phase, mine, theirs):
        total = mine[chip].astype(F32)
        for step in reversed(CHIP_ORDER):
            j = chip_peer(*step)
            remote(phase, mine.at[j], theirs.at[j], j, j, attn_id(me)).wait_recv()
            total = total + theirs[j].astype(F32)
        return total * inverse

    total = summed(REDUCE, tx7, rx7)
    mixed = total[:, 256:384]
    half = silu(mixed) * pltpu.roll(mixed, 64, axis=1)
    right = jnp.where(iota((CAP, 128), 1) < 64, 0, 1)
    half = jnp.where(right == lax.rem(chip, 2), half, 0.0)
    activated = jnp.concatenate([silu(total[:, 0:128]) * total[:, 128:256], half], axis=1).astype(BF16)
    tx8[...] = activated
    rx8[0, chip] = activated
    to_chips(ACT, lambda j: tx8, rx8.at[0, chip])
    remote(FORWARD, tx8, rx8.at[1, chip], chip, chip, attn_id(sibling)).start()
    total = summed(REDUCE_B, tx7b, rx7b)
    activated = (silu(total[:, 0:128]) * total[:, 128:256]).astype(BF16)
    tx8b[...] = activated
    rx8b[0, chip] = activated
    to_chips(ACT_B, lambda j: tx8b, rx8b.at[0, chip])
    remote(FORWARD_B, tx8b, rx8b.at[1, chip], chip, chip, attn_id(sibling)).start()
    l_wd.wait()

    def forward_pair(dx, phase, onward, src, dst):
        for dy in (0, 1):
            if (dx, dy) != (0, 0):
                j = chip_peer(dx, dy)
                remote(phase, src, dst.at[0, j], j, j, attn_id(me)).wait_recv()
                remote(onward, dst.at[0, j], dst.at[1, j], j, j, attn_id(sibling)).start()

    def down_pair(dx):
        p = lax.rem(at_x + dx, 4)
        for j in (2 * p, 2 * p + 1):
            remote(FORWARD, tx8, rx8.at[1, j], j, j, attn_id(me)).wait_recv()
            remote(FORWARD_B, tx8b, rx8b.at[1, j], j, j, attn_id(me)).wait_recv()
        parts = []
        for side in range(2):
            a, b = rx8[side, 2 * p], rx8[side, 2 * p + 1]
            middle = (a[:, 128:256].astype(F32) + b[:, 128:256].astype(F32)).astype(BF16)
            parts.append(jnp.concatenate(
                [a[:, 0:128], rx8b[side, 2 * p], middle, b[:, 0:128], rx8b[side, 2 * p + 1]], axis=1
            ))
        lanes = pl.ds(pl.multiple_of(640 * p, 128), 640)
        return dot_nt(jnp.concatenate(parts, axis=0), wd[:, lanes])

    result = jnp.zeros((2 * CAP, W), F32)
    for dx in far_first:
        forward_pair(dx, ACT, FORWARD, tx8, rx8)
    for k, dx in enumerate(far_first):
        forward_pair(dx, ACT_B, FORWARD_B, tx8b, rx8b)
        if k > 0:
            result = result + down_pair(far_first[k - 1])
    result = result + down_pair(0)
    result = (result * route).astype(BF16)
    added = dot(spread[:, 0:2 * CAP], result)
    tx9[...] = fold(padded(added).reshape(NG, 8, 512)).astype(BF16)
    rx9[g_me] = tx9[g_me]
    spread_group(BACK, lambda peer: tx9.at[peer], rx9)

    def sent(phase, every):
        remote(phase, every, every, 0, 0, attn_id(me)).wait_send()

    for phase, dst in ((QUERY, rx1), (PARTIAL, rx2), (HEADS_FIRST, rx3.at[0]), (HEADS_OUT, rx3.at[1]), (PROJ, rx4), (ROWS_IN, rx5), (STATS, rx6), (BACK, rx9)):
        sent(phase, dst.at[pl.ds(0, 15)])
    sent(SIBLING, txs)
    sent(REDUCE, tx7.at[pl.ds(0, CHIPS - 1)])
    sent(ACT, rx8.at[0, pl.ds(0, CHIPS - 1)])
    sent(FORWARD, rx8.at[0])
    sent(REDUCE_B, tx7b.at[pl.ds(0, CHIPS - 1)])
    sent(ACT_B, rx8b.at[0, pl.ds(0, CHIPS - 1)])
    sent(FORWARD_B, rx8b.at[0])
    await_all(BACK, rx9)
    final = hidden_v[...] + unfold(jnp.sum(rx9[...].astype(F32), axis=0))
    out[0] = final[0:4, 0:W].astype(BF16)
    out[1] = final[4:8, 0:W].astype(BF16)


def on_device(
    queries, new_pairs, kv_pool, table_first, table_second, lengths, migrations, residual,
    out_proj, norm_gain, router, routes, gate_weight, up_weight, down_weight,
):
    vmem, smem = pltpu.VMEM, pltpu.SMEM
    return pl.pallas_call(
        body,
        out_shape=jax.ShapeDtypeStruct((2, 4, W), BF16),
        in_specs=[pl.BlockSpec(memory_space=pltpu.HBM)] * 15,
        out_specs=pl.BlockSpec(memory_space=pltpu.VMEM),
        scratch_shapes=[
            smem((2, 4), jnp.int32), smem((1, 16), jnp.int32),
            vmem((2, 4, 1024), BF16), vmem((2, 4, 512), BF16), vmem((LOCAL, PAGE, 2 * HD), BF16),
            vmem((4, 16), jnp.int32), vmem((4, 16), jnp.int32), vmem((2, 64, W), BF16), vmem((W, 1024), BF16),
            vmem((W,), BF16), vmem((1, W), BF16), vmem((3, 2, 64), jnp.int32),
            vmem((W, 2560), BF16), vmem((W, 2560), BF16), vmem((W, 2560), BF16),
            pltpu.SemaphoreType.DMA((15,)), pltpu.SemaphoreType.DMA((15,)), pltpu.SemaphoreType.DMA((15, 16)), pltpu.SemaphoreType.REGULAR((4,)),
            vmem((NA, 16, 384), BF16), vmem((NA, 16, 384), BF16),
            vmem((NA, 16, 384), BF16), vmem((NA, 16, 384), BF16),
            vmem((2, 16, HD), BF16), vmem((2, NA, 16, HD), BF16),
            vmem((NG, 16, 256), BF16), vmem((NG, 16, 256), BF16),
            vmem((16, 256), BF16), vmem((NG, 16, 256), BF16),
            vmem((8, 128), F32), vmem((NA, 8, 128), F32),
            vmem((CHIPS, CAP, 640), BF16), vmem((CHIPS, CAP, 640), BF16),
            vmem((CHIPS, CAP, 384), BF16), vmem((CHIPS, CAP, 384), BF16),
            vmem((CHIPS, CAP, 256), BF16), vmem((CHIPS, CAP, 256), BF16),
            vmem((CAP, 256), BF16), vmem((2, CHIPS, CAP, 256), BF16),
            vmem((CAP, 128), BF16), vmem((2, CHIPS, CAP, 128), BF16),
            vmem((NG, 16, 256), BF16), vmem((NG, 16, 256), BF16),
            vmem((2, 32, TOKENS), F32), vmem((16, 512), F32), vmem((8, 512), F32), vmem((2 * CAP, W), BF16), vmem((128, 512), BF16),
            vmem((128, 128), F32), vmem((128, 128), BF16), vmem((8, 512), BF16), vmem((CHIPS, CAP, 640), F32),
        ],
        compiler_params=pltpu.CompilerParams(
            collective_id=0, has_side_effects=True, vmem_limit_bytes=60 * 1024 * 1024
        ),
        name="layer",
    )(
        queries, new_pairs, kv_pool, table_first, table_second, lengths, migrations, residual,
        out_proj.T, norm_gain, router.T, routes.transpose(2, 0, 1), gate_weight, up_weight, down_weight[0].T,
    )


def solution(mesh):
    return jax.shard_map(
        on_device,
        mesh=mesh,
        in_specs=(
            P(None, "attn", ("ffn", "tp")),
            P(None, "attn", None),
            P("attn", None, None),
            P("attn", None),
            P("attn", None),
            P(None, "attn"),
            P("attn", None),
            P(None, None, "attn"),
            P(("ffn", "tp"), "attn"),
            P("attn"),
            P("attn", "ffn"),
            P(),
            P("ffn", "attn", "tp"),
            P("ffn", "attn", "tp"),
            P("ffn", "tp", "attn"),
        ),
        out_specs=P(None, ("ffn", "tp"), "attn"),
        check_vma=False,
    )
```
